32 devices in a mesh: band: 8 (over z, y), fft: 4 (over x, core).
Axes of the slice: x: 2, y: 2, z: 4, core: 2. Of those that a mesh axis runs over, the one named last changes fastest.
Arguments:
- wavefunctions: bfloat16 [8, 176, 30976], P('band', 'fft'), may hold values from -6 to 6
- band_occ: int32 [8], P('band'), may hold values from 0 to 2
Outputs:
- exchange_term: float32 [8, 176, 30976], P('band', 'fft')
The draws below stay inside these ranges and needn't reach their ends.
All inputs are finite; a program needn't handle non-finite values.
Results may differ from the reference program's by a relative error of at most 0.0003.
Values may be sent and summed in bfloat16 or wider, within the bound.
A program may use at most 128 MiB of HBM per device.

```python
import jax
import jax.numpy as jnp
from jax import lax

NG = 176
BAND_DEV = 1
CYCLE_STEPS = 2
BANDS = 8
N_BAND = 8


def with_ends(values, rng, smallest, top_value):
    longest = values.shape.index(max(values.shape))
    spots = []
    for shift in (0, 1):
        where = [jax.random.randint(jax.random.fold_in(rng, axis), (), 0, length) for axis, length in enumerate(values.shape)]
        where[longest] = (where[longest] + shift) % values.shape[longest]
        spots.append(tuple(where))
    return values.at[spots[0]].set(smallest).at[spots[1]].set(top_value)


def steps_of(key, dims, cuts, low, largest):
    factor_of, own = 1.0, jax.random.fold_in(key, 6)
    for axis_at, blocks in cuts:
        steps = jnp.exp(jax.random.uniform(jax.random.fold_in(own, axis_at), (blocks,), jnp.float32, low / len(cuts), largest / len(cuts)))
        factor_of = factor_of * jnp.repeat(steps, dims[axis_at] // blocks).reshape([-1 if axis == axis_at else 1 for axis in range(len(dims))])
    return factor_of


def bell_draw(own_key, dims, deviation, limit, cuts=(), held_as=jnp.bfloat16):
    array = jax.random.normal(own_key, dims, jnp.float32) * deviation
    if len(cuts) > 0:
        array = steps_of(own_key, dims, cuts, -0.22, 0.18) * array
    return jnp.clip(array, min=-limit, max=limit).astype(held_as)


def setup_inputs(seed: int = 0) -> dict:
    splits = jax.random.split(jax.random.key(seed), 3)
    return {
        "wavefunctions": bell_draw(splits[0], (BANDS, NG, NG * NG), 1.0, 6.0, ((0, 8), (1, 4))),
        "band_occ": with_ends(jax.random.randint(splits[1], (BANDS,), 0, 3), jax.random.fold_in(splits[1], 1), 0, 2).astype(jnp.int32),
    }


def truncated_profile(grid_size):
    indices = jnp.arange(grid_size, dtype=jnp.int32)
    folded = jnp.minimum(indices, grid_size - indices).astype(jnp.float32)
    squares = folded * folded
    summed = squares[:, None, None] + squares[None, :, None] + squares[None, None, :]
    safe_sum = jnp.maximum(summed, 1.0)
    radius = jnp.sqrt(safe_sum)
    return jnp.where(summed > 0.5, 2.0 * (1.0 - jnp.cos(jnp.pi * radius)) / (jnp.pi * jnp.pi * safe_sum), 1.0)

def pair_potential(density, kernel):
    spectrum = jnp.fft.rfftn(density, axes=(1, 2, 3))
    return jnp.fft.irfftn(spectrum * kernel, s=density.shape[1:], axes=(1, 2, 3)).astype(jnp.float32)

def reference(wavefunctions, band_occ):
    group_count = N_BAND
    fields = wavefunctions.reshape(group_count, BAND_DEV, NG, NG, NG)
    weights = band_occ.astype(jnp.float32).reshape(group_count, BAND_DEV)
    kernel = truncated_profile(NG)[:, :, :NG // 2 + 1] * (0.25 * float(NG) ** 1.5)
    collected = jnp.zeros((group_count, BAND_DEV, NG, NG, NG), jnp.float32)
    for cycle_step in range(1, CYCLE_STEPS + 1):

        def block_terms(group_id):
            source_group = (group_id - cycle_step) % group_count
            home_block = fields[group_id].astype(jnp.float32)
            visitor = fields[source_group].astype(jnp.float32)
            home_occ = weights[group_id]
            visitor_occ = weights[source_group]
            density = (home_block[:, None] * visitor[None]).reshape(BAND_DEV * BAND_DEV, NG, NG, NG)
            potential = pair_potential(density, kernel).reshape(BAND_DEV, BAND_DEV, NG, NG, NG)
            own_terms = -0.5 * lax.optimization_barrier(jnp.sum(potential * (visitor_occ[:, None, None, None] * visitor)[None], axis=1))
            return_terms = -0.5 * lax.optimization_barrier(jnp.sum(potential * (home_occ[:, None, None, None] * home_block)[:, None], axis=0))
            return (own_terms, return_terms)
        own_terms, return_terms = lax.map(block_terms, jnp.arange(group_count, dtype=jnp.int32))
        collected = collected + own_terms + jnp.roll(return_terms, -cycle_step, axis=0)
    return collected.reshape(group_count * BAND_DEV, NG, NG * NG)
```

```python
import functools

import jax
import jax.numpy as jnp
import numpy as np
from jax import lax
from jax.experimental import pallas as pl
from jax.experimental.pallas import tpu as pltpu
from jax.sharding import PartitionSpec as P

LANES = 256
LEVELS = 32000.0
STEPS_PER_OCTAVE = 64.0
F32 = jnp.float32
BF16 = jnp.bfloat16
VMEM_BYTES = 60 * 1024 * 1024


def round_up(value, multiple):
    return -(-value // multiple) * multiple


def cas_table(grid_size):
    indices = np.arange(grid_size)
    phases = (indices[:, None] * indices[None, :] % grid_size) * (2.0 * np.pi / grid_size)
    return np.cos(phases) + np.sin(phases)


def high_low(table):
    table = table.astype(np.float32)
    high = table.astype(BF16)
    low = (table - high.astype(np.float32)).astype(BF16)
    return jnp.asarray(high), jnp.asarray(low)


def spread_rows(table, blocks, slab, block_rows):
    spread = np.zeros((blocks * block_rows, table.shape[1]))
    for block in range(blocks):
        spread[block * block_rows : block * block_rows + slab] = table[block * slab : (block + 1) * slab]
    return spread


def folded_squares(indices, grid_size):
    folded = jnp.minimum(indices, grid_size - indices).astype(F32)
    return folded * folded


def truncated_kernel(grid_size, slab, rows):
    indices = jnp.arange(grid_size, dtype=jnp.int32)
    squares = folded_squares(indices, grid_size)
    lanes = folded_squares(jnp.minimum(jnp.arange(LANES, dtype=jnp.int32), grid_size), grid_size)
    own_rows = lax.axis_index("fft") * slab + jnp.arange(rows, dtype=jnp.int32)
    row_squares = folded_squares(own_rows, grid_size)
    summed = row_squares[:, None, None] + squares[None, :, None] + lanes[None, None, :]
    safe_sum = jnp.maximum(summed, 1.0)
    radius = jnp.sqrt(safe_sum)
    profile = jnp.where(
        summed > 0.5, 2.0 * (1.0 - jnp.cos(jnp.pi * radius)) / (jnp.pi * jnp.pi * safe_sum), 1.0
    )
    return profile * (0.25 / float(grid_size) ** 1.5)


def parts_of(value):
    high = value.astype(BF16)
    return high, (value - high.astype(F32)).astype(BF16)


def dot(left, right):
    return jnp.dot(left, right, preferred_element_type=F32)


def times_table(value, table):
    high, low = parts_of(value)
    return dot(high, table[0]) + (dot(low, table[0]) + dot(high, table[1]))


def table_times(table, value):
    high, low = parts_of(value)
    return dot(table[0], high) + (dot(table[0], low) + dot(table[1], high))


def exponent_of(largest):
    return jnp.ceil(jnp.log2(jnp.maximum(largest, 1e-30)) * STEPS_PER_OCTAVE)


def step_of(exponent):
    return jnp.exp2(exponent * (1.0 / STEPS_PER_OCTAVE))


def coded(value, slab):
    exponent = exponent_of(jnp.max(jnp.abs(value), axis=-2, keepdims=True))
    scaled = jnp.round(value * (LEVELS / step_of(exponent)))
    row = lax.broadcasted_iota(jnp.int32, value.shape, value.ndim - 2)
    return jnp.where(row == slab, exponent, scaled)


def decoded(code, slab):
    return code * (step_of(code[..., slab : slab + 1, :]) * (1.0 / LEVELS))


def to_wire(code):
    return code.astype(jnp.int32).astype(jnp.int16)


def from_wire(wire):
    return wire.astype(jnp.int32).astype(F32)


def shared_lanes(first, second):
    lane = lax.broadcasted_iota(jnp.int32, first.shape, first.ndim - 1)
    return jnp.where(lane < 64, first, pltpu.roll(second, 64, second.ndim - 1))


def unshared(both):
    lane = lax.broadcasted_iota(jnp.int32, both.shape, both.ndim - 1)
    first = jnp.where(lane < 64, both, 0.0)
    second = jnp.where(lane < 64, pltpu.roll(both, 64, both.ndim - 1), 0.0)
    return first, second


def forward_kernel(slab, blocks, block_rows, a_ref, b_ref, zh, zl, yh, yl, out_ref, buf):
    planes, grid_size = a_ref.shape[0], a_ref.shape[1]
    half = out_ref.shape[1] // 3
    z_table, y_table = (zh[...], zl[...]), (yh[...], yl[...])

    @pl.loop(0, planes // 8)
    def _(chunk):
        rows = pl.ds(pl.multiple_of(chunk * 8, 8), 8)
        density = a_ref[rows].astype(F32) * b_ref[rows].astype(F32)
        along_z = times_table(density.reshape(8 * grid_size, grid_size), z_table)
        along_z = along_z.reshape(8, grid_size, LANES)
        along_y = jnp.stack([table_times(y_table, along_z[i]) for i in range(8)])
        buf[:, rows, :] = jnp.transpose(along_y, (1, 0, 2))

    for block in range(blocks):

        @pl.loop(0, half)
        def _(row):
            first = coded(buf[block * block_rows + row], slab)
            second = coded(buf[block * block_rows + half + row], slab)
            out_ref[block, row] = to_wire(first[:, :128])
            out_ref[block, half + row] = to_wire(second[:, :128])
            out_ref[block, 2 * half + row] = to_wire(shared_lanes(first[:, 128:], second[:, 128:]))


def filter_kernel(slab, in_ref, w_ref, fh, fl, ih, il, out_ref):
    blocks, half, planes = in_ref.shape[0], in_ref.shape[1] // 3, in_ref.shape[2]
    forward, inverse = (fh[...], fl[...]), (ih[...], il[...])

    @pl.loop(0, half)
    def _(row):
        upper = unshared(from_wire(in_ref[:, 2 * half + row]))
        codes = []
        for i in range(2):
            at = row + i * half
            code = jnp.concatenate([from_wire(in_ref[:, at]), upper[i]], axis=-1)
            field = decoded(code, slab).reshape(blocks * planes, LANES)
            spectrum = table_times(forward, field) * w_ref[at]
            filtered = table_times(inverse, spectrum).reshape(blocks, planes, LANES)
            code = coded(filtered, slab)
            out_ref[:, at] = to_wire(code[..., :128])
            codes.append(code[..., 128:])
        out_ref[:, 2 * half + row] = to_wire(shared_lanes(codes[0], codes[1]))


def back_kernel(slab, blocks, block_rows, with_swapped, *refs):
    if with_swapped:
        in_ref, a_ref, b_ref, occ, swapped, zh, zl, yh, yl, own_ref, ret_ref, buf, ret = refs
    else:
        in_ref, a_ref, b_ref, occ, zh, zl, yh, yl, own_ref, ret_ref, buf, ret = refs
    planes, grid_size = a_ref.shape[0], a_ref.shape[1]
    half = in_ref.shape[1] // 3
    halfx = (ret_ref.shape[0] - 2) // 3
    z_table, y_table = (zh[...], zl[...]), (yh[...], yl[...])
    home, visitor = -0.5 * occ[0], -0.5 * occ[1]

    for block in range(blocks):
        base = block * block_rows
        buf[base + 2 * half : base + block_rows] = jnp.zeros(
            (block_rows - 2 * half, planes, LANES), F32
        )

        @pl.loop(0, half)
        def _(row):
            upper = unshared(from_wire(in_ref[block, 2 * half + row]))
            for i in range(2):
                at = row + i * half
                code = jnp.concatenate([from_wire(in_ref[block, at]), upper[i]], axis=-1)
                buf[base + at] = decoded(code, slab)

    def chunk_at(chunk, largest):
        rows = pl.ds(pl.multiple_of(chunk * 8, 8), 8)
        mixed = jnp.transpose(buf[:, rows, :], (1, 0, 2))
        along_y = jnp.stack([table_times(y_table, mixed[i]) for i in range(8)])
        field = times_table(along_y.reshape(8 * grid_size, LANES), z_table)
        field = field.reshape(8, grid_size, LANES)[..., :grid_size]
        own_ref[rows] = field * b_ref[rows].astype(F32) * visitor
        terms = field * a_ref[rows].astype(F32) * home
        ret[rows] = terms
        if with_swapped:
            return largest
        return jnp.maximum(largest, jnp.max(jnp.abs(terms), axis=0))

    largest = lax.fori_loop(0, planes // 8, chunk_at, jnp.zeros((grid_size, grid_size), F32))

    if with_swapped:
        add_own, add_ret = occ[2], occ[3]
        step = plane_steps(swapped, halfx)

        def add_at(row, largest):
            upper = unshared(from_wire(swapped[2 * halfx + row]))
            for i in range(2):
                at = row + i * halfx
                code = jnp.concatenate([from_wire(swapped[at]), upper[i]], axis=-1)
                value = (code * step)[:, :grid_size]
                own_ref[at] = own_ref[at] + value * add_own
                total = ret[at] + value * add_ret
                ret[at] = total
                largest = jnp.maximum(largest, jnp.abs(total))
            return largest

        largest = lax.fori_loop(0, halfx, add_at, largest)

    exponent = exponent_of(widened(largest))
    scale = LEVELS / step_of(exponent)

    @pl.loop(0, halfx)
    def _(row):
        codes = []
        for i in range(2):
            code = jnp.round(widened(ret[row + i * halfx]) * scale)
            ret_ref[row + i * halfx] = to_wire(code[:, :128])
            codes.append(code[:, 128:])
        ret_ref[2 * halfx + row] = to_wire(shared_lanes(codes[0], codes[1]))

    ret_ref[3 * halfx] = to_wire(exponent[:, :128])
    ret_ref[3 * halfx + 1] = to_wire(exponent[:, 128:])


def widened(plane):
    pad = jnp.zeros((plane.shape[0], LANES - plane.shape[1]), F32)
    return jnp.concatenate([plane, pad], axis=-1)


def plane_steps(wire_ref, halfx):
    exponent = jnp.concatenate(
        [from_wire(wire_ref[3 * halfx]), from_wire(wire_ref[3 * halfx + 1])], axis=-1
    )
    return step_of(exponent) * (1.0 / LEVELS)


def total_kernel(first_ref, second_ref, arrived, out_ref):
    grid_size = first_ref.shape[1]
    halfx = (arrived.shape[0] - 2) // 3
    step = plane_steps(arrived, halfx)

    @pl.loop(0, halfx)
    def _(row):
        upper = unshared(from_wire(arrived[2 * halfx + row]))
        for i in range(2):
            at = row + i * halfx
            code = jnp.concatenate([from_wire(arrived[at]), upper[i]], axis=-1)
            out_ref[at] = first_ref[at] + second_ref[at] + (code * step)[:, :grid_size]


def call(kernel, out_shape, scratch, name, flops, *operands, smem=()):
    specs = [
        pl.BlockSpec(memory_space=pltpu.SMEM if at in smem else pltpu.VMEM)
        for at in range(len(operands))
    ]
    single = pl.BlockSpec(memory_space=pltpu.VMEM)
    bytes_moved = sum(o.size * o.dtype.itemsize for o in operands)
    return pl.pallas_call(
        kernel,
        out_shape=out_shape,
        in_specs=specs,
        out_specs=[single] * len(out_shape) if isinstance(out_shape, list) else single,
        scratch_shapes=scratch,
        compiler_params=pltpu.CompilerParams(vmem_limit_bytes=VMEM_BYTES),
        cost_estimate=pl.CostEstimate(flops=flops, bytes_accessed=bytes_moved, transcendentals=0),
        name=name,
    )(*operands)


def exchange(wire):
    return lax.all_to_all(wire, "fft", split_axis=0, concat_axis=0, tiled=True)


def shards(wavefunctions, band_occ):
    slab = wavefunctions.shape[1]
    blocks = lax.axis_size("fft")
    bands = lax.axis_size("band")
    grid_size = slab * blocks
    planes = round_up(slab + 1, 16)
    block_rows = round_up(slab, 8)
    half = (slab + 1) // 2
    ky_rows = blocks * block_rows

    table = cas_table(grid_size)
    lanes_table = np.zeros((grid_size, LANES))
    lanes_table[:, :grid_size] = table
    square_table = np.zeros((LANES, LANES))
    square_table[:grid_size, :grid_size] = table
    to_ky = spread_rows(table, blocks, slab, block_rows)
    to_x = spread_rows(table, blocks, slab, planes)
    z_forward, z_back = high_low(lanes_table), high_low(square_table)
    y_forward, y_back = high_low(to_ky), high_low(to_ky.T)
    x_forward, x_back = high_low(to_x.T), high_low(to_x)
    profile = truncated_kernel(grid_size, slab, 2 * half)

    occupied = band_occ.astype(BF16)
    upward = [(i, (i + 2) % bands) for i in range(bands)]
    downward = [(i, (i - 2) % bands) for i in range(bands)]
    swap = [(i, i ^ 1) for i in range(bands)]
    is_odd = lax.axis_index("band") % 2 == 1

    wide = lambda psi: jnp.pad(psi[0], ((0, planes - slab), (0, 0))).reshape(
        planes, grid_size, grid_size
    )
    far, far_occ = lax.ppermute((wavefunctions, occupied), "band", upward)
    near, near_occ = lax.ppermute(
        (jnp.where(is_odd, far, wavefunctions), jnp.where(is_odd, far_occ, occupied)), "band", swap
    )
    home = wide(wavefunctions)
    flops = 12 * planes * grid_size**3

    def forward(visitor):
        return call(
            functools.partial(forward_kernel, slab, blocks, block_rows),
            jax.ShapeDtypeStruct((blocks, 3 * half, planes, 128), jnp.int16),
            [pltpu.VMEM((ky_rows, planes, LANES), F32)],
            "density_to_ky_kz",
            flops,
            home,
            visitor,
            *z_forward,
            *y_forward,
        )

    def filtered(wire):
        return call(
            functools.partial(filter_kernel, slab),
            jax.ShapeDtypeStruct(wire.shape, jnp.int16),
            [],
            "filter_along_x",
            flops,
            wire,
            profile,
            *x_forward,
            *x_back,
        )

    def back(wire, visitor, factors, swapped=None):
        extra = [] if swapped is None else [swapped]
        return call(
            functools.partial(back_kernel, slab, blocks, block_rows, swapped is not None),
            [
                jax.ShapeDtypeStruct((planes, grid_size, grid_size), F32),
                jax.ShapeDtypeStruct((3 * half + 2, grid_size, 128), jnp.int16),
            ],
            [
                pltpu.VMEM((ky_rows, planes, LANES), F32),
                pltpu.VMEM((planes, grid_size, grid_size), F32),
            ],
            "potential_terms",
            flops,
            wire,
            home,
            visitor,
            factors,
            *extra,
            *z_back,
            *y_back,
            smem=(3,),
        )

    far_field, near_field = wide(far), wide(near)
    odd = is_odd.astype(F32)
    home_occ = occupied.astype(F32)[0]
    near_factors = jnp.stack([home_occ, near_occ.astype(F32)[0], 1.0 - odd, odd])
    far_factors = jnp.stack([home_occ, far_occ.astype(F32)[0], 1.0 - odd, odd])

    near_wire = exchange(forward(near_field))
    far_wire = exchange(forward(far_field))
    near_wire = exchange(filtered(near_wire))
    far_wire = exchange(filtered(far_wire))
    near_own, near_return = back(near_wire, near_field, near_factors)
    swapped = lax.ppermute(near_return, "band", swap)
    far_own, far_return = back(far_wire, far_field, far_factors, swapped)
    arrived = lax.ppermute(far_return, "band", downward)
    total = call(
        total_kernel,
        jax.ShapeDtypeStruct((planes, grid_size, grid_size), F32),
        [],
        "total_terms",
        3 * planes * grid_size**2,
        near_own,
        far_own,
        arrived,
    )
    return total[:slab].reshape(1, slab, grid_size * grid_size)


def solution(mesh):
    in_specs = (P("band", "fft", None), P("band"))
    out_specs = P("band", "fft", None)
    return jax.shard_map(shards, mesh=mesh, in_specs=in_specs, out_specs=out_specs, check_vma=False)
```

```python
import functools

import jax
import jax.numpy as jnp
import numpy as np
from jax import lax
from jax.experimental import pallas as pl
from jax.experimental.pallas import tpu as pltpu
from jax.sharding import PartitionSpec as P

LANES = 256
LEVELS = 32000.0
STEPS_PER_OCTAVE = 64.0
F32 = jnp.float32
BF16 = jnp.bfloat16
VMEM_BYTES = 60 * 1024 * 1024


def round_up(value, multiple):
    return -(-value // multiple) * multiple


def cas_table(grid_size):
    indices = np.arange(grid_size)
    phases = (indices[:, None] * indices[None, :] % grid_size) * (2.0 * np.pi / grid_size)
    return np.cos(phases) + np.sin(phases)


def high_low(table):
    table = table.astype(np.float32)
    high = table.astype(BF16)
    low = (table - high.astype(np.float32)).astype(BF16)
    return jnp.asarray(high), jnp.asarray(low)


def spread_rows(table, blocks, slab, block_rows):
    spread = np.zeros((blocks * block_rows, table.shape[1]))
    for block in range(blocks):
        spread[block * block_rows : block * block_rows + slab] = table[block * slab : (block + 1) * slab]
    return spread


def folded_squares(indices, grid_size):
    folded = jnp.minimum(indices, grid_size - indices).astype(F32)
    return folded * folded


def truncated_kernel(grid_size, slab, rows):
    indices = jnp.arange(grid_size, dtype=jnp.int32)
    squares = folded_squares(indices, grid_size)
    lanes = folded_squares(jnp.minimum(jnp.arange(LANES, dtype=jnp.int32), grid_size), grid_size)
    own_rows = lax.axis_index("fft") * slab + jnp.arange(rows, dtype=jnp.int32)
    row_squares = folded_squares(own_rows, grid_size)
    summed = row_squares[:, None, None] + squares[None, :, None] + lanes[None, None, :]
    safe_sum = jnp.maximum(summed, 1.0)
    radius = jnp.sqrt(safe_sum)
    profile = jnp.where(
        summed > 0.5, 2.0 * (1.0 - jnp.cos(jnp.pi * radius)) / (jnp.pi * jnp.pi * safe_sum), 1.0
    )
    return profile * (0.25 / float(grid_size) ** 1.5)


def parts_of(value):
    high = value.astype(BF16)
    return high, (value - high.astype(F32)).astype(BF16)


def dot(left, right):
    return jnp.dot(left, right, preferred_element_type=F32)


def times_table(value, table):
    high, low = parts_of(value)
    return dot(high, table[0]) + (dot(low, table[0]) + dot(high, table[1]))


def table_times(table, value):
    high, low = parts_of(value)
    return dot(table[0], high) + (dot(table[0], low) + dot(table[1], high))


def exponent_of(largest):
    return jnp.ceil(jnp.log2(jnp.maximum(largest, 1e-30)) * STEPS_PER_OCTAVE)


def step_of(exponent):
    return jnp.exp2(exponent * (1.0 / STEPS_PER_OCTAVE))


def coded(value, slab):
    exponent = exponent_of(jnp.max(jnp.abs(value), axis=-2, keepdims=True))
    scaled = jnp.round(value * (LEVELS / step_of(exponent)))
    row = lax.broadcasted_iota(jnp.int32, value.shape, value.ndim - 2)
    return jnp.where(row == slab, exponent, scaled)


def decoded(code, slab):
    return code * (step_of(code[..., slab : slab + 1, :]) * (1.0 / LEVELS))


def to_wire(code):
    return code.astype(jnp.int32).astype(jnp.int16)


def from_wire(wire):
    return wire.astype(jnp.int32).astype(F32)


def shared_lanes(first, second):
    lane = lax.broadcasted_iota(jnp.int32, first.shape, first.ndim - 1)
    return jnp.where(lane < 64, first, pltpu.roll(second, 64, second.ndim - 1))


def unshared(both):
    lane = lax.broadcasted_iota(jnp.int32, both.shape, both.ndim - 1)
    first = jnp.where(lane < 64, both, 0.0)
    second = jnp.where(lane < 64, pltpu.roll(both, 64, both.ndim - 1), 0.0)
    return first, second


def group_slices(group_lanes, grid_size):
    for row in range(group_lanes // grid_size):
        first, offset = divmod(row * grid_size, 128)
        yield row, first, offset, -(-(offset + grid_size) // 128)


def forward_kernel(slab, blocks, block_rows, a_ref, b_ref, zh, zl, yh, yl, out_ref, dens, rows_z, rows_y, buf):
    planes, cells = a_ref.shape
    grid_size = rows_z.shape[0]
    half = out_ref.shape[1] // 3
    group_lanes = 8 * grid_size
    z_table, y_table = (zh[...], zl[...]), (yh[...], yl[...])

    @pl.loop(0, cells // group_lanes)
    def _(group):
        lanes = pl.ds(pl.multiple_of(group * group_lanes, 128), group_lanes)
        dens[:, lanes] = a_ref[:, lanes].astype(F32) * b_ref[:, lanes].astype(F32)

    @pl.loop(0, planes // 16)
    def _(chunk):
        rows = pl.ds(pl.multiple_of(chunk * 16, 16), 16)

        @pl.loop(0, cells // group_lanes)
        def _(group):
            lanes = pl.ds(pl.multiple_of(group * group_lanes, 128), group_lanes)
            flat = dens[rows, lanes]
            for row, first, offset, tiles in group_slices(group_lanes, grid_size):
                window = flat[:, first * 128 : (first + tiles) * 128]
                if offset:
                    window = pltpu.roll(window, tiles * 128 - offset, 1)
                rows_z[group * 8 + row] = window[:, :LANES]

        @pl.loop(0, 2)
        def _(part):
            count = grid_size // 2
            at = pl.ds(pl.multiple_of(part * count, 8), count)
            along_z = times_table(rows_z[at].reshape(count * 16, LANES), z_table)
            rows_y[:, at, :] = jnp.transpose(along_z.reshape(count, 16, LANES), (1, 0, 2))

        @pl.loop(0, 2)
        def _(part):
            along_y = jnp.stack([table_times(y_table, rows_y[part * 8 + i]) for i in range(8)])
            at = pl.ds(pl.multiple_of(chunk * 16 + part * 8, 8), 8)
            buf[:, at, :] = jnp.transpose(along_y, (1, 0, 2))

    for block in range(blocks):

        @pl.loop(0, half)
        def _(row):
            first = coded(buf[block * block_rows + row], slab)
            second = coded(buf[block * block_rows + half + row], slab)
            out_ref[block, row] = to_wire(first[:, :128])
            out_ref[block, half + row] = to_wire(second[:, :128])
            out_ref[block, 2 * half + row] = to_wire(shared_lanes(first[:, 128:], second[:, 128:]))


def filter_kernel(slab, in_ref, w_ref, fh, fl, ih, il, out_ref):
    blocks, half, planes = in_ref.shape[0], in_ref.shape[1] // 3, in_ref.shape[2]
    forward, inverse = (fh[...], fl[...]), (ih[...], il[...])

    @pl.loop(0, half)
    def _(row):
        upper = unshared(from_wire(in_ref[:, 2 * half + row]))
        codes = []
        for i in range(2):
            at = row + i * half
            code = jnp.concatenate([from_wire(in_ref[:, at]), upper[i]], axis=-1)
            field = decoded(code, slab).reshape(blocks * planes, LANES)
            spectrum = table_times(forward, field) * w_ref[at]
            filtered = table_times(inverse, spectrum).reshape(blocks, planes, LANES)
            code = coded(filtered, slab)
            out_ref[:, at] = to_wire(code[..., :128])
            codes.append(code[..., 128:])
        out_ref[:, 2 * half + row] = to_wire(shared_lanes(codes[0], codes[1]))


def back_kernel(
    slab, blocks, block_rows, in_ref, a_ref, b_ref, occ, zh, zl, yh, yl, own_ref, ret_ref, buf, rows_z, field
):
    planes, cells = a_ref.shape
    grid_size = rows_z.shape[0]
    half = in_ref.shape[1] // 3
    group_lanes = 8 * grid_size
    z_table, y_table = (zh[...], zl[...]), (yh[...], yl[...])
    home, visitor = -0.5 * occ[0], -0.5 * occ[1]

    for block in range(blocks):
        base = block * block_rows
        buf[base + 2 * half : base + block_rows] = jnp.zeros(
            (block_rows - 2 * half, planes, LANES), F32
        )

        @pl.loop(0, half)
        def _(row):
            upper = unshared(from_wire(in_ref[block, 2 * half + row]))
            for i in range(2):
                at = row + i * half
                code = jnp.concatenate([from_wire(in_ref[block, at]), upper[i]], axis=-1)
                buf[base + at] = decoded(code, slab)

    @pl.loop(0, planes // 8)
    def _(chunk):
        rows = pl.ds(pl.multiple_of(chunk * 8, 8), 8)
        mixed = jnp.transpose(buf[:, rows, :], (1, 0, 2))
        along_y = jnp.stack([table_times(y_table, mixed[i]) for i in range(8)])
        along_z = times_table(along_y.reshape(8 * grid_size, LANES), z_table)
        rows_z[...] = jnp.transpose(along_z.reshape(8, grid_size, LANES), (1, 0, 2))

        @pl.loop(0, cells // group_lanes)
        def _(group):
            tiles_of = [None] * (group_lanes // 128)
            for row, first, offset, tiles in group_slices(group_lanes, grid_size):
                window = rows_z[group * 8 + row]
                if tiles * 128 > LANES:
                    window = jnp.concatenate([window, jnp.zeros((8, tiles * 128 - LANES), F32)], axis=1)
                if offset:
                    window = pltpu.roll(window, offset, 1)
                for tile in range(tiles):
                    piece = window[:, tile * 128 : (tile + 1) * 128]
                    before = tiles_of[first + tile]
                    tiles_of[first + tile] = piece if before is None else before + piece
            lanes = pl.ds(pl.multiple_of(group * group_lanes, 128), group_lanes)
            field[rows, lanes] = jnp.concatenate(tiles_of, axis=1)

    @pl.loop(0, cells // group_lanes)
    def _(group):
        lanes = pl.ds(pl.multiple_of(group * group_lanes, 128), group_lanes)
        potential = field[:, lanes]
        own_ref[:, lanes] = potential * b_ref[:, lanes].astype(F32) * visitor
        terms = potential * a_ref[:, lanes].astype(F32) * home
        ret_ref[:, lanes] = to_wire(coded(terms, slab))


def call(kernel, out_shape, scratch, name, flops, *operands, smem=()):
    specs = [
        pl.BlockSpec(memory_space=pltpu.SMEM if at in smem else pltpu.VMEM)
        for at in range(len(operands))
    ]
    single = pl.BlockSpec(memory_space=pltpu.VMEM)
    bytes_moved = sum(o.size * o.dtype.itemsize for o in operands)
    return pl.pallas_call(
        kernel,
        out_shape=out_shape,
        in_specs=specs,
        out_specs=[single] * len(out_shape) if isinstance(out_shape, list) else single,
        scratch_shapes=scratch,
        compiler_params=pltpu.CompilerParams(vmem_limit_bytes=VMEM_BYTES),
        cost_estimate=pl.CostEstimate(flops=flops, bytes_accessed=bytes_moved, transcendentals=0),
        name=name,
    )(*operands)


def exchange(wire):
    return lax.all_to_all(wire, "fft", split_axis=0, concat_axis=0, tiled=True)


def shards(wavefunctions, band_occ):
    slab = wavefunctions.shape[1]
    blocks = lax.axis_size("fft")
    bands = lax.axis_size("band")
    grid_size = slab * blocks
    planes = round_up(slab + 1, 16)
    block_rows = round_up(slab, 8)
    half = (slab + 1) // 2
    ky_rows = blocks * block_rows

    table = cas_table(grid_size)
    square_table = np.zeros((LANES, LANES))
    square_table[:grid_size, :grid_size] = table
    to_ky = spread_rows(table, blocks, slab, block_rows)
    to_x = spread_rows(table, blocks, slab, planes)
    z_back = high_low(square_table)
    y_forward, y_back = high_low(to_ky), high_low(to_ky.T)
    x_forward, x_back = high_low(to_x.T), high_low(to_x)
    profile = truncated_kernel(grid_size, slab, 2 * half)

    occupied = band_occ.astype(BF16)
    upward = [(i, (i + 2) % bands) for i in range(bands)]
    downward = [(i, (i - 2) % bands) for i in range(bands)]
    swap = [(i, i ^ 1) for i in range(bands)]
    is_odd = lax.axis_index("band") % 2 == 1

    cells = grid_size * grid_size
    home = jnp.pad(wavefunctions[0], ((0, planes - slab), (0, 0)))
    home_first, home_second = home[:, : cells // 2], home[:, cells // 2 :]
    far_occ = lax.ppermute(occupied, "band", upward)
    near_occ = lax.ppermute(jnp.where(is_odd, far_occ, occupied), "band", swap)
    far_first = lax.ppermute(home_first, "band", upward)
    home_later, far_first = lax.optimization_barrier((home_second, far_first))
    far_second = lax.ppermute(home_later, "band", upward)
    near_first = lax.ppermute(jnp.where(is_odd, far_first, home_first), "band", swap)
    near_second = lax.ppermute(jnp.where(is_odd, far_second, home_second), "band", swap)
    far_field = jnp.concatenate([far_first, far_second], axis=1)
    near_field = jnp.concatenate([near_first, near_second], axis=1)
    far_field, profile = lax.optimization_barrier((far_field, profile))
    flops = 12 * planes * grid_size**3

    def forward(visitor):
        return call(
            functools.partial(forward_kernel, slab, blocks, block_rows),
            jax.ShapeDtypeStruct((blocks, 3 * half, planes, 128), jnp.int16),
            [
                pltpu.VMEM((planes, cells), F32),
                pltpu.VMEM((grid_size, 16, LANES), F32),
                pltpu.VMEM((16, grid_size, LANES), F32),
                pltpu.VMEM((ky_rows, planes, LANES), F32),
            ],
            "density_to_ky_kz",
            flops,
            home,
            visitor,
            *z_back,
            *y_forward,
        )

    def filtered(wire):
        return call(
            functools.partial(filter_kernel, slab),
            jax.ShapeDtypeStruct(wire.shape, jnp.int16),
            [],
            "filter_along_x",
            flops,
            wire,
            profile,
            *x_forward,
            *x_back,
        )

    def back(wire, visitor, factors):
        return call(
            functools.partial(back_kernel, slab, blocks, block_rows),
            [
                jax.ShapeDtypeStruct((planes, cells), F32),
                jax.ShapeDtypeStruct((planes, cells), jnp.int16),
            ],
            [
                pltpu.VMEM((ky_rows, planes, LANES), F32),
                pltpu.VMEM((grid_size, 8, LANES), F32),
                pltpu.VMEM((planes, cells), F32),
            ],
            "potential_terms",
            flops,
            wire,
            home,
            visitor,
            factors,
            *z_back,
            *y_back,
            smem=(3,),
        )

    home_occ = occupied.astype(F32)[0]
    near_factors = jnp.stack([home_occ, near_occ.astype(F32)[0]])
    far_factors = jnp.stack([home_occ, far_occ.astype(F32)[0]])

    far_wire = exchange(forward(far_field))
    near_wire = exchange(forward(near_field))
    far_wire = exchange(filtered(far_wire))
    near_wire = exchange(filtered(near_wire))
    far_own, far_return = back(far_wire, far_field, far_factors)
    far_arrived = lax.ppermute(far_return, "band", downward)
    near_own, near_return = back(near_wire, near_field, near_factors)
    near_arrived = lax.ppermute(near_return, "band", [(i, (i - 1) % bands) for i in range(bands)])

    def terms_of(arrived):
        code = arrived.astype(F32)
        return code[:slab] * (step_of(code[slab : slab + 1]) * (1.0 / LEVELS))

    total = far_own[:slab] + near_own[:slab] + terms_of(far_arrived) + terms_of(near_arrived)
    return total[None]


def solution(mesh):
    in_specs = (P("band", "fft", None), P("band"))
    out_specs = P("band", "fft", None)
    return jax.shard_map(shards, mesh=mesh, in_specs=in_specs, out_specs=out_specs, check_vma=False)
```

```python
import functools

import jax
import jax.numpy as jnp
import numpy as np
from jax import lax
from jax.experimental import pallas as pl
from jax.experimental.pallas import tpu as pltpu
from jax.sharding import PartitionSpec as P

LANES = 256
LEVELS = 32000.0
STEPS_PER_OCTAVE = 64.0
F32 = jnp.float32
BF16 = jnp.bfloat16
VMEM_BYTES = 60 * 1024 * 1024


def round_up(value, multiple):
    return -(-value // multiple) * multiple


def cas_table(grid_size):
    indices = np.arange(grid_size)
    phases = (indices[:, None] * indices[None, :] % grid_size) * (2.0 * np.pi / grid_size)
    return np.cos(phases) + np.sin(phases)


def high_low(table, axis):
    table = table.astype(np.float32)
    high = table.astype(BF16)
    low = (table - high.astype(np.float32)).astype(BF16)
    return jnp.asarray(np.concatenate([high, high, low], axis=axis))


def spread_rows(table, blocks, slab, block_rows):
    spread = np.zeros((blocks * block_rows, table.shape[1]))
    for block in range(blocks):
        spread[block * block_rows : block * block_rows + slab] = table[block * slab : (block + 1) * slab]
    return spread


def folded_squares(indices, grid_size):
    folded = jnp.minimum(indices, grid_size - indices).astype(F32)
    return folded * folded


def truncated_kernel(grid_size, slab, rows):
    indices = jnp.arange(grid_size, dtype=jnp.int32)
    squares = folded_squares(indices, grid_size)
    lanes = folded_squares(jnp.minimum(jnp.arange(LANES, dtype=jnp.int32), grid_size), grid_size)
    own_rows = lax.axis_index("fft") * slab + jnp.arange(rows, dtype=jnp.int32)
    row_squares = folded_squares(own_rows, grid_size)
    summed = row_squares[:, None, None] + squares[None, :, None] + lanes[None, None, :]
    safe_sum = jnp.maximum(summed, 1.0)
    radius = jnp.sqrt(safe_sum)
    profile = jnp.where(
        summed > 0.5, 2.0 * (1.0 - jnp.cos(jnp.pi * radius)) / (jnp.pi * jnp.pi * safe_sum), 1.0
    )
    return profile * (0.25 / float(grid_size) ** 1.5)


def parts_of(value):
    high = value.astype(BF16)
    return high, (value - high.astype(F32)).astype(BF16)


def dot(left, right):
    return jnp.dot(left, right, preferred_element_type=F32)


def times_table(value, table):
    high, low = parts_of(value)
    return dot(jnp.concatenate([high, low, high], axis=1), table)


def table_times(table, value):
    high, low = parts_of(value)
    return dot(table, jnp.concatenate([high, low, high], axis=0))


def exponent_of(largest):
    return jnp.ceil(jnp.log2(jnp.maximum(largest, 1e-30)) * STEPS_PER_OCTAVE)


def step_of(exponent):
    return jnp.exp2(exponent * (1.0 / STEPS_PER_OCTAVE))


def coded(value, slab):
    exponent = exponent_of(jnp.max(jnp.abs(value), axis=-2, keepdims=True))
    scaled = jnp.round(value * (LEVELS / step_of(exponent)))
    row = lax.broadcasted_iota(jnp.int32, value.shape, value.ndim - 2)
    return jnp.where(row == slab, exponent, scaled)


def decoded(code, slab):
    return code * (step_of(code[..., slab : slab + 1, :]) * (1.0 / LEVELS))


def to_wire(code):
    return code.astype(jnp.int32).astype(jnp.int16)


def from_wire(wire):
    return wire.astype(jnp.int32).astype(F32)


def shared_lanes(first, second):
    lane = lax.broadcasted_iota(jnp.int32, first.shape, first.ndim - 1)
    return jnp.where(lane < 64, first, pltpu.roll(second, 64, second.ndim - 1))


def unshared(both):
    lane = lax.broadcasted_iota(jnp.int32, both.shape, both.ndim - 1)
    first = jnp.where(lane < 64, both, 0.0)
    second = jnp.where(lane < 64, pltpu.roll(both, 64, both.ndim - 1), 0.0)
    return first, second


def group_slices(group_lanes, grid_size):
    for row in range(group_lanes // grid_size):
        first, offset = divmod(row * grid_size, 128)
        yield row, first, offset, -(-(offset + grid_size) // 128)


def forward_kernel(slab, blocks, block_rows, a_ref, b_ref, z_ref, y_ref, out_ref, dens, rows_z, rows_y, buf):
    planes, cells = a_ref.shape
    grid_size = rows_z.shape[0]
    half = out_ref.shape[1] // 3
    group_lanes = 8 * grid_size
    z_table, y_table = z_ref[...], y_ref[...]

    @pl.loop(0, cells // group_lanes)
    def _(group):
        lanes = pl.ds(pl.multiple_of(group * group_lanes, 128), group_lanes)
        dens[:, lanes] = a_ref[:, lanes].astype(F32) * b_ref[:, lanes].astype(F32)

    @pl.loop(0, planes // 16)
    def _(chunk):
        rows = pl.ds(pl.multiple_of(chunk * 16, 16), 16)

        @pl.loop(0, cells // group_lanes, unroll=2)
        def _(group):
            lanes = pl.ds(pl.multiple_of(group * group_lanes, 128), group_lanes)
            flat = dens[rows, lanes]
            for row, first, offset, tiles in group_slices(group_lanes, grid_size):
                window = flat[:, first * 128 : (first + tiles) * 128]
                if offset:
                    window = pltpu.roll(window, tiles * 128 - offset, 1)
                rows_z[group * 8 + row] = window[:, :LANES]

        @pl.loop(0, 2)
        def _(part):
            count = grid_size // 2
            at = pl.ds(pl.multiple_of(part * count, 8), count)
            along_z = times_table(rows_z[at].reshape(count * 16, LANES), z_table)
            rows_y[:, at, :] = jnp.transpose(along_z.reshape(count, 16, LANES), (1, 0, 2))

        @pl.loop(0, 2)
        def _(part):
            along_y = jnp.stack([table_times(y_table, rows_y[part * 8 + i]) for i in range(8)])
            at = pl.ds(pl.multiple_of(chunk * 16 + part * 8, 8), 8)
            buf[:, at, :] = jnp.transpose(along_y, (1, 0, 2))

    @pl.loop(0, half)
    def _(row):
        for block in range(blocks):
            first = coded(buf[block * block_rows + row], slab)
            second = coded(buf[block * block_rows + half + row], slab)
            out_ref[block, row] = to_wire(first[:, :128])
            out_ref[block, half + row] = to_wire(second[:, :128])
            out_ref[block, 2 * half + row] = to_wire(shared_lanes(first[:, 128:], second[:, 128:]))


def filter_kernel(slab, in_ref, w_ref, forward_ref, inverse_ref, out_ref):
    blocks, half, planes = in_ref.shape[0], in_ref.shape[1] // 3, in_ref.shape[2]
    forward, inverse = forward_ref[...], inverse_ref[...]

    @pl.loop(0, half, unroll=2)
    def _(row):
        upper = unshared(from_wire(in_ref[:, 2 * half + row]))
        codes = []
        for i in range(2):
            at = row + i * half
            code = jnp.concatenate([from_wire(in_ref[:, at]), upper[i]], axis=-1)
            field = decoded(code, slab).reshape(blocks * planes, LANES)
            spectrum = table_times(forward, field) * w_ref[at]
            filtered = table_times(inverse, spectrum).reshape(blocks, planes, LANES)
            code = coded(filtered, slab)
            out_ref[:, at] = to_wire(code[..., :128])
            codes.append(code[..., 128:])
        out_ref[:, 2 * half + row] = to_wire(shared_lanes(codes[0], codes[1]))


def back_kernel(
    slab, blocks, block_rows, in_ref, a_ref, b_ref, occ, z_ref, y_ref, own_ref, ret_ref, buf, rows_z, field
):
    planes, cells = a_ref.shape
    grid_size = rows_z.shape[0]
    half = in_ref.shape[1] // 3
    group_lanes = 8 * grid_size
    z_table, y_table = z_ref[...], y_ref[...]
    home, visitor = -0.5 * occ[0], -0.5 * occ[1]

    for block in range(blocks):
        base = block * block_rows
        buf[base + 2 * half : base + block_rows] = jnp.zeros(
            (block_rows - 2 * half, planes, LANES), F32
        )

    @pl.loop(0, half)
    def _(row):
        for block in range(blocks):
            base = block * block_rows
            upper = unshared(from_wire(in_ref[block, 2 * half + row]))
            for i in range(2):
                at = row + i * half
                code = jnp.concatenate([from_wire(in_ref[block, at]), upper[i]], axis=-1)
                buf[base + at] = decoded(code, slab)

    @pl.loop(0, planes // 8)
    def _(chunk):
        rows = pl.ds(pl.multiple_of(chunk * 8, 8), 8)
        mixed = jnp.transpose(buf[:, rows, :], (1, 0, 2))
        along_y = jnp.stack([table_times(y_table, mixed[i]) for i in range(8)])
        along_z = times_table(along_y.reshape(8 * grid_size, LANES), z_table)
        rows_z[...] = jnp.transpose(along_z.reshape(8, grid_size, LANES), (1, 0, 2))

        @pl.loop(0, cells // group_lanes, unroll=2)
        def _(group):
            tiles_of = [None] * (group_lanes // 128)
            for row, first, offset, tiles in group_slices(group_lanes, grid_size):
                window = rows_z[group * 8 + row]
                if tiles * 128 > LANES:
                    window = jnp.concatenate([window, jnp.zeros((8, tiles * 128 - LANES), F32)], axis=1)
                if offset:
                    window = pltpu.roll(window, offset, 1)
                for tile in range(tiles):
                    piece = window[:, tile * 128 : (tile + 1) * 128]
                    before = tiles_of[first + tile]
                    tiles_of[first + tile] = piece if before is None else before + piece
            lanes = pl.ds(pl.multiple_of(group * group_lanes, 128), group_lanes)
            field[rows, lanes] = jnp.concatenate(tiles_of, axis=1)

    @pl.loop(0, cells // group_lanes)
    def _(group):
        lanes = pl.ds(pl.multiple_of(group * group_lanes, 128), group_lanes)
        potential = field[:, lanes]
        own_ref[:, lanes] = potential * b_ref[:, lanes].astype(F32) * visitor
        terms = potential * a_ref[:, lanes].astype(F32) * home
        ret_ref[:, lanes] = to_wire(coded(terms, slab))


def call(kernel, out_shape, scratch, name, flops, *operands, smem=()):
    specs = [
        pl.BlockSpec(memory_space=pltpu.SMEM if at in smem else pltpu.VMEM)
        for at in range(len(operands))
    ]
    single = pl.BlockSpec(memory_space=pltpu.VMEM)
    bytes_moved = sum(o.size * o.dtype.itemsize for o in operands)
    return pl.pallas_call(
        kernel,
        out_shape=out_shape,
        in_specs=specs,
        out_specs=[single] * len(out_shape) if isinstance(out_shape, list) else single,
        scratch_shapes=scratch,
        compiler_params=pltpu.CompilerParams(vmem_limit_bytes=VMEM_BYTES),
        cost_estimate=pl.CostEstimate(flops=flops, bytes_accessed=bytes_moved, transcendentals=0),
        name=name,
    )(*operands)


def exchange(wire):
    return lax.all_to_all(wire, "fft", split_axis=0, concat_axis=0, tiled=True)


def shards(wavefunctions, band_occ):
    slab = wavefunctions.shape[1]
    blocks = lax.axis_size("fft")
    bands = lax.axis_size("band")
    grid_size = slab * blocks
    planes = round_up(slab + 1, 16)
    block_rows = round_up(slab, 8)
    half = (slab + 1) // 2
    ky_rows = blocks * block_rows

    table = cas_table(grid_size)
    square_table = np.zeros((LANES, LANES))
    square_table[:grid_size, :grid_size] = table
    to_ky = spread_rows(table, blocks, slab, block_rows)
    to_x = spread_rows(table, blocks, slab, planes)
    z_table = high_low(square_table, 0)
    y_forward, y_back = high_low(to_ky, 1), high_low(to_ky.T, 1)
    x_forward, x_back = high_low(to_x.T, 1), high_low(to_x, 1)
    profile = truncated_kernel(grid_size, slab, 2 * half)

    occupied = band_occ.astype(BF16)
    upward = [(i, (i + 2) % bands) for i in range(bands)]
    downward = [(i, (i - 2) % bands) for i in range(bands)]
    swap = [(i, i ^ 1) for i in range(bands)]
    is_odd = lax.axis_index("band") % 2 == 1

    cells = grid_size * grid_size
    home = jnp.pad(wavefunctions[0], ((0, planes - slab), (0, 0)))
    home_first, home_second = home[:, : cells // 2], home[:, cells // 2 :]
    far_occ = lax.ppermute(occupied, "band", upward)
    near_occ = lax.ppermute(jnp.where(is_odd, far_occ, occupied), "band", swap)
    far_first = lax.ppermute(home_first, "band", upward)
    home_later, far_first = lax.optimization_barrier((home_second, far_first))
    far_second = lax.ppermute(home_later, "band", upward)
    near_first = lax.ppermute(jnp.where(is_odd, far_first, home_first), "band", swap)
    near_second = lax.ppermute(jnp.where(is_odd, far_second, home_second), "band", swap)
    far_field = jnp.concatenate([far_first, far_second], axis=1)
    near_field = jnp.concatenate([near_first, near_second], axis=1)
    far_field, profile = lax.optimization_barrier((far_field, profile))
    flops = 12 * planes * grid_size**3

    def forward(visitor):
        return call(
            functools.partial(forward_kernel, slab, blocks, block_rows),
            jax.ShapeDtypeStruct((blocks, 3 * half, planes, 128), jnp.int16),
            [
                pltpu.VMEM((planes, cells), F32),
                pltpu.VMEM((grid_size, 16, LANES), F32),
                pltpu.VMEM((16, grid_size, LANES), F32),
                pltpu.VMEM((ky_rows, planes, LANES), F32),
            ],
            "density_to_ky_kz",
            flops,
            home,
            visitor,
            z_table,
            y_forward,
        )

    def filtered(wire):
        return call(
            functools.partial(filter_kernel, slab),
            jax.ShapeDtypeStruct(wire.shape, jnp.int16),
            [],
            "filter_along_x",
            flops,
            wire,
            profile,
            x_forward,
            x_back,
        )

    def back(wire, visitor, factors):
        return call(
            functools.partial(back_kernel, slab, blocks, block_rows),
            [
                jax.ShapeDtypeStruct((planes, cells), F32),
                jax.ShapeDtypeStruct((planes, cells), jnp.int16),
            ],
            [
                pltpu.VMEM((ky_rows, planes, LANES), F32),
                pltpu.VMEM((grid_size, 8, LANES), F32),
                pltpu.VMEM((planes, cells), F32),
            ],
            "potential_terms",
            flops,
            wire,
            home,
            visitor,
            factors,
            z_table,
            y_back,
            smem=(3,),
        )

    home_occ = occupied.astype(F32)[0]
    near_factors = jnp.stack([home_occ, near_occ.astype(F32)[0]])
    far_factors = jnp.stack([home_occ, far_occ.astype(F32)[0]])

    far_wire = exchange(forward(far_field))
    near_wire = exchange(forward(near_field))
    far_wire = exchange(filtered(far_wire))
    near_wire = exchange(filtered(near_wire))
    far_own, far_return = back(far_wire, far_field, far_factors)
    far_arrived = lax.ppermute(far_return, "band", downward)
    near_own, near_return = back(near_wire, near_field, near_factors)
    near_arrived = lax.ppermute(near_return, "band", [(i, (i - 1) % bands) for i in range(bands)])

    def terms_of(arrived):
        code = arrived.astype(F32)
        return code[:slab] * (step_of(code[slab : slab + 1]) * (1.0 / LEVELS))

    total = far_own[:slab] + near_own[:slab] + terms_of(far_arrived) + terms_of(near_arrived)
    return total[None]


def solution(mesh):
    in_specs = (P("band", "fft", None), P("band"))
    out_specs = P("band", "fft", None)
    return jax.shard_map(shards, mesh=mesh, in_specs=in_specs, out_specs=out_specs, check_vma=False)
```

```python
import functools

import jax
import jax.numpy as jnp
import numpy as np
from jax import lax
from jax.experimental import pallas as pl
from jax.experimental.pallas import tpu as pltpu
from jax.sharding import PartitionSpec as P

LANES = 256
CHUNK = 15
ROWS = 16
LEVELS = 32000.0
STEPS_PER_OCTAVE = 64.0
F32 = jnp.float32
BF16 = jnp.bfloat16
VMEM_BYTES = 60 * 1024 * 1024


def round_up(value, multiple):
    return -(-value // multiple) * multiple


def cas_table(grid_size):
    indices = np.arange(grid_size)
    phases = (indices[:, None] * indices[None, :] % grid_size) * (2.0 * np.pi / grid_size)
    return np.cos(phases) + np.sin(phases)


def high_low(table, axis):
    table = table.astype(np.float32)
    high = table.astype(BF16)
    low = (table - high.astype(np.float32)).astype(BF16)
    return jnp.asarray(np.concatenate([high, high, low], axis=axis))


def spread_rows(table, blocks, slab, block_rows):
    spread = np.zeros((blocks * block_rows, table.shape[1]))
    for block in range(blocks):
        spread[block * block_rows : block * block_rows + slab] = table[block * slab : (block + 1) * slab]
    return spread


def spread_planes(table, blocks, slab):
    planes = round_up(slab, CHUNK) // CHUNK * ROWS
    spread = np.zeros((blocks * planes, table.shape[1]))
    for plane in range(blocks * slab):
        block, own = divmod(plane, slab)
        spread[block * planes + own // CHUNK * ROWS + own % CHUNK] = table[plane]
    return spread


def folded_squares(indices, grid_size):
    folded = jnp.minimum(indices, grid_size - indices).astype(F32)
    return folded * folded


def sine_of_half_turns(turns):
    angle = turns * jnp.pi
    square = angle * angle
    series = jnp.full_like(square, 1.0 / 6227020800.0)
    for factor in (-1.0 / 39916800.0, 1.0 / 362880.0, -1.0 / 5040.0, 1.0 / 120.0, -1.0 / 6.0, 1.0):
        series = series * square + factor
    return angle * series


def truncated_kernel(grid_size, slab, rows):
    lanes = folded_squares(jnp.minimum(jnp.arange(LANES, dtype=jnp.int32), grid_size), grid_size)
    folded = jnp.arange(round_up(grid_size // 2 + 1, 8), dtype=jnp.int32).astype(F32)
    squares = folded * folded
    own_rows = lax.axis_index("fft") * slab + jnp.arange(rows, dtype=jnp.int32)
    row_squares = folded_squares(own_rows, grid_size)
    summed = row_squares[:, None, None] + squares[None, :, None] + lanes[None, None, :]
    safe_sum = jnp.maximum(summed, 1.0)
    half_radius = 0.5 * jnp.sqrt(safe_sum)
    sine = sine_of_half_turns(half_radius - jnp.round(half_radius))
    profile = jnp.where(summed > 0.5, 4.0 * sine * sine / (jnp.pi * jnp.pi * safe_sum), 1.0)
    return profile * (0.25 / float(grid_size) ** 1.5)


def parts_of(value):
    high = value.astype(BF16)
    return high, (value - high.astype(F32)).astype(BF16)


def dot(left, right):
    return jnp.dot(left, right, preferred_element_type=F32)


def times_table(value, table):
    high, low = parts_of(value)
    return dot(jnp.concatenate([high, low, high], axis=1), table)


def table_times(table, value):
    high, low = parts_of(value)
    return dot(table, jnp.concatenate([high, low, high], axis=0))


def exponent_of(largest):
    return jnp.ceil(jnp.log2(jnp.maximum(largest, 1e-30)) * STEPS_PER_OCTAVE)


def step_of(exponent):
    return jnp.exp2(exponent * (1.0 / STEPS_PER_OCTAVE))


def coded(value):
    exponent = exponent_of(jnp.max(jnp.abs(value), axis=-2, keepdims=True))
    scaled = jnp.round(value * (LEVELS / step_of(exponent)))
    row = lax.broadcasted_iota(jnp.int32, value.shape, value.ndim - 2)
    return jnp.where(row == CHUNK, exponent, scaled)


def decoded(code):
    return code * (step_of(code[..., CHUNK:, :]) * (1.0 / LEVELS))


def to_wire(code):
    return code.astype(jnp.int32).astype(jnp.int16)


def from_wire(wire):
    return wire.astype(jnp.int32).astype(F32)


def shared_lanes(first, second):
    lane = lax.broadcasted_iota(jnp.int32, first.shape, first.ndim - 1)
    return jnp.where(lane < 64, first, pltpu.roll(second, 64, second.ndim - 1))


def unshared(both):
    lane = lax.broadcasted_iota(jnp.int32, both.shape, both.ndim - 1)
    first = jnp.where(lane < 64, both, 0.0)
    second = jnp.where(lane < 64, pltpu.roll(both, 64, both.ndim - 1), 0.0)
    return first, second


def group_slices(group_lanes, grid_size):
    for row in range(group_lanes // grid_size):
        first, offset = divmod(row * grid_size, 128)
        yield row, first, offset, -(-(offset + grid_size) // 128)


def forward_kernel(blocks, block_rows, a_ref, b_ref, z_ref, y_ref, out_ref, rows_z, rows_y, buf):
    cells = a_ref.shape[1]
    grid_size = rows_z.shape[0]
    half = out_ref.shape[1] // 3
    group_lanes = 8 * grid_size
    z_table, y_table = z_ref[...], y_ref[...]

    @pl.loop(0, cells // group_lanes, unroll=2)
    def _(group):
        lanes = pl.ds(pl.multiple_of(group * group_lanes, 128), group_lanes)
        flat = a_ref[:, lanes].astype(F32) * b_ref[:, lanes].astype(F32)
        for row, first, offset, tiles in group_slices(group_lanes, grid_size):
            window = flat[:, first * 128 : (first + tiles) * 128]
            if offset:
                window = pltpu.roll(window, tiles * 128 - offset, 1)
            rows_z[group * 8 + row] = window[:, :LANES]

    @pl.loop(0, 2)
    def _(part):
        count = grid_size // 2
        at = pl.ds(pl.multiple_of(part * count, 8), count)
        along_z = times_table(rows_z[at].reshape(count * ROWS, LANES), z_table)
        rows_y[:, at, :] = jnp.transpose(along_z.reshape(count, ROWS, LANES), (1, 0, 2))

    @pl.loop(0, 2)
    def _(part):
        along_y = jnp.stack([table_times(y_table, rows_y[part * 8 + i]) for i in range(8)])
        at = pl.ds(pl.multiple_of(part * 8, 8), 8)
        buf[:, at, :] = jnp.transpose(along_y, (1, 0, 2))

    @pl.loop(0, half)
    def _(row):
        for block in range(blocks):
            first = coded(buf[block * block_rows + row])
            second = coded(buf[block * block_rows + half + row])
            out_ref[block, row] = to_wire(first[:, :128])
            out_ref[block, half + row] = to_wire(second[:, :128])
            out_ref[block, 2 * half + row] = to_wire(shared_lanes(first[:, 128:], second[:, 128:]))


def filter_kernel(chunks, *refs):
    in_refs, (w_ref, forward_ref, inverse_ref, out_ref) = refs[:chunks], refs[chunks:]
    blocks, half = out_ref.shape[0], out_ref.shape[1] // 3
    middle = forward_ref.shape[0] // 2
    forward, inverse = forward_ref[...], inverse_ref[...]

    @pl.loop(0, half, unroll=2)
    def _(row):
        upper = [unshared(from_wire(ref[:, 2 * half + row])) for ref in in_refs]
        codes = []
        for i in range(2):
            at = row + i * half
            fields = [
                decoded(jnp.concatenate([from_wire(ref[:, at]), upper[chunk][i]], axis=-1))
                for chunk, ref in enumerate(in_refs)
            ]
            field = jnp.concatenate(fields, axis=1).reshape(blocks * chunks * ROWS, LANES)
            lower_w = w_ref[at, :middle]
            rows = lax.broadcasted_iota(jnp.int32, lower_w.shape, 0)
            upper_w = jnp.where(rows == 0, w_ref[at, middle : middle + 1], lower_w)
            spectrum = table_times(forward, field) * jnp.concatenate([lower_w, upper_w], axis=0)
            filtered = table_times(inverse, spectrum).reshape(blocks, chunks, ROWS, LANES)
            code = coded(filtered).reshape(blocks, chunks * ROWS, LANES)
            out_ref[:, at] = to_wire(code[..., :128])
            codes.append(code[..., 128:])
        out_ref[:, 2 * half + row] = to_wire(shared_lanes(codes[0], codes[1]))


def back_kernel(blocks, block_rows, in_ref, a_ref, b_ref, occ, z_ref, y_ref, own_ref, ret_ref, buf, rows_z, field):
    cells = a_ref.shape[1]
    grid_size = rows_z.shape[0]
    half = in_ref.shape[1] // 3
    group_lanes = 8 * grid_size
    z_table, y_table = z_ref[...], y_ref[...]
    home, visitor = -0.5 * occ[0], -0.5 * occ[1]

    for block in range(blocks):
        base = block * block_rows
        buf[base + 2 * half : base + block_rows] = jnp.zeros((block_rows - 2 * half, ROWS, LANES), F32)

    @pl.loop(0, half)
    def _(row):
        for block in range(blocks):
            base = block * block_rows
            upper = unshared(from_wire(in_ref[block, 2 * half + row]))
            for i in range(2):
                at = row + i * half
                code = jnp.concatenate([from_wire(in_ref[block, at]), upper[i]], axis=-1)
                buf[base + at] = decoded(code)

    @pl.loop(0, 2)
    def _(part):
        rows = pl.ds(pl.multiple_of(part * 8, 8), 8)
        mixed = jnp.transpose(buf[:, rows, :], (1, 0, 2))
        along_y = jnp.stack([table_times(y_table, mixed[i]) for i in range(8)])
        along_z = times_table(along_y.reshape(8 * grid_size, LANES), z_table)
        rows_z[...] = jnp.transpose(along_z.reshape(8, grid_size, LANES), (1, 0, 2))

        @pl.loop(0, cells // group_lanes, unroll=2)
        def _(group):
            tiles_of = [None] * (group_lanes // 128)
            for row, first, offset, tiles in group_slices(group_lanes, grid_size):
                window = rows_z[group * 8 + row]
                if tiles * 128 > LANES:
                    window = jnp.concatenate([window, jnp.zeros((8, tiles * 128 - LANES), F32)], axis=1)
                if offset:
                    window = pltpu.roll(window, offset, 1)
                for tile in range(tiles):
                    piece = window[:, tile * 128 : (tile + 1) * 128]
                    before = tiles_of[first + tile]
                    tiles_of[first + tile] = piece if before is None else before + piece
            lanes = pl.ds(pl.multiple_of(group * group_lanes, 128), group_lanes)
            field[rows, lanes] = jnp.concatenate(tiles_of, axis=1)

    @pl.loop(0, cells // group_lanes)
    def _(group):
        lanes = pl.ds(pl.multiple_of(group * group_lanes, 128), group_lanes)
        potential = field[:, lanes]
        own_ref[:, lanes] = potential * b_ref[:, lanes].astype(F32) * visitor
        terms = potential * a_ref[:, lanes].astype(F32) * home
        ret_ref[:, lanes] = to_wire(coded(terms))


def total_kernel(chunks, *refs):
    out_ref = refs[-1]
    slab = out_ref.shape[1]
    for chunk in range(chunks):
        first, second, third, fourth = refs[4 * chunk : 4 * chunk + 4]
        total = first[...] + second[...]
        total = total + decoded(from_wire(third[...])) + decoded(from_wire(fourth[...]))
        start = chunk * CHUNK
        stop = min(start + CHUNK, slab)
        out_ref[0, start:stop] = total[: stop - start]


def call(kernel, out_shape, scratch, name, flops, operands, in_specs=None):
    single = pl.BlockSpec(memory_space=pltpu.VMEM)
    bytes_moved = sum(o.size * o.dtype.itemsize for o in operands)
    return pl.pallas_call(
        kernel,
        grid=(1,) if in_specs else (),
        out_shape=out_shape,
        in_specs=in_specs or [single] * len(operands),
        out_specs=[single] * len(out_shape) if isinstance(out_shape, list) else single,
        scratch_shapes=scratch,
        compiler_params=pltpu.CompilerParams(vmem_limit_bytes=VMEM_BYTES),
        cost_estimate=pl.CostEstimate(flops=flops, bytes_accessed=bytes_moved, transcendentals=0),
        name=name,
    )(*operands)


def exchange(wire):
    return lax.all_to_all(wire, "fft", split_axis=0, concat_axis=0, tiled=True)


def shards(wavefunctions, band_occ):
    _, slab, cells = wavefunctions.shape
    blocks = lax.axis_size("fft")
    bands = lax.axis_size("band")
    grid_size = slab * blocks
    chunks = round_up(slab, CHUNK) // CHUNK
    planes = chunks * ROWS
    block_rows = round_up(slab, 8)
    half = (slab + 1) // 2
    ky_rows = blocks * block_rows

    table = cas_table(grid_size)
    square_table = np.zeros((LANES, LANES))
    square_table[:grid_size, :grid_size] = table
    to_ky = spread_rows(table, blocks, slab, block_rows)
    middle = grid_size // 2
    kx_order = np.concatenate([np.arange(middle), [middle], grid_size - np.arange(1, middle)])
    to_x = spread_planes(table[:, kx_order], blocks, slab)
    z_table = high_low(square_table, 0)
    y_forward, y_back = high_low(to_ky, 1), high_low(to_ky.T, 1)
    x_forward, x_back = high_low(to_x.T, 1), high_low(to_x, 1)
    profile = truncated_kernel(grid_size, slab, 2 * half)

    occupied = band_occ.astype(BF16)
    upward = [(i, (i + 2) % bands) for i in range(bands)]
    downward = [(i, (i - 2) % bands) for i in range(bands)]
    downward_one = [(i, (i - 1) % bands) for i in range(bands)]
    swap = [(i, i ^ 1) for i in range(bands)]
    is_odd = lax.axis_index("band") % 2 == 1

    def chunk_of(chunk):
        piece = wavefunctions[0, chunk * CHUNK : (chunk + 1) * CHUNK]
        return jnp.pad(piece, ((0, ROWS - piece.shape[0]), (0, 0)))

    home = [chunk_of(chunk) for chunk in range(chunks)]
    far_occ = lax.ppermute(occupied, "band", upward)
    near_occ = lax.ppermute(jnp.where(is_odd, far_occ, occupied), "band", swap)
    far, near = [], []
    for chunk in range(chunks):
        sent = home[chunk]
        if far:
            sent, far[-1] = lax.optimization_barrier((sent, far[-1]))
        far.append(lax.ppermute(sent, "band", upward))
    far[0], profile = lax.optimization_barrier((far[0], profile))
    for chunk in range(chunks):
        near.append(lax.ppermute(jnp.where(is_odd, far[chunk], home[chunk]), "band", swap))
    flops = 12 * ROWS * grid_size**3

    def forward(chunk, visitor):
        return call(
            functools.partial(forward_kernel, blocks, block_rows),
            jax.ShapeDtypeStruct((blocks, 3 * half, ROWS, 128), jnp.int16),
            [
                pltpu.VMEM((grid_size, ROWS, LANES), F32),
                pltpu.VMEM((ROWS, grid_size, LANES), F32),
                pltpu.VMEM((ky_rows, ROWS, LANES), F32),
            ],
            "density_to_ky_kz",
            flops,
            [home[chunk], visitor[chunk], z_table, y_forward],
        )

    def filtered(wires):
        return call(
            functools.partial(filter_kernel, chunks),
            jax.ShapeDtypeStruct((blocks, 3 * half, planes, 128), jnp.int16),
            [],
            "filter_along_x",
            chunks * flops,
            [*wires, profile, x_forward, x_back],
        )

    def back(wire, chunk, visitor, factors):
        whole = pl.BlockSpec(memory_space=pltpu.VMEM)
        piece = pl.BlockSpec((blocks, 3 * half, ROWS, 128), lambda i: (0, 0, chunk, 0))
        return call(
            functools.partial(back_kernel, blocks, block_rows),
            [
                jax.ShapeDtypeStruct((ROWS, cells), F32),
                jax.ShapeDtypeStruct((ROWS, cells), jnp.int16),
            ],
            [
                pltpu.VMEM((ky_rows, ROWS, LANES), F32),
                pltpu.VMEM((grid_size, 8, LANES), F32),
                pltpu.VMEM((ROWS, cells), F32),
            ],
            "potential_terms",
            flops,
            [wire, home[chunk], visitor[chunk], factors, z_table, y_back],
            [piece, whole, whole, pl.BlockSpec(memory_space=pltpu.SMEM), whole, whole],
        )

    home_occ = occupied.astype(F32)[0]
    near_factors = jnp.stack([home_occ, near_occ.astype(F32)[0]])
    far_factors = jnp.stack([home_occ, far_occ.astype(F32)[0]])

    far_wires = [exchange(forward(chunk, far)) for chunk in range(chunks)]
    near_wires = [exchange(forward(chunk, near)) for chunk in range(chunks)]
    far_wire = exchange(filtered(far_wires))
    near_wire = exchange(filtered(near_wires))
    far_parts = [back(far_wire, chunk, far, far_factors) for chunk in range(chunks)]
    near_parts = [back(near_wire, chunk, near, near_factors) for chunk in range(chunks)]
    operands = []
    for (far_own, far_return), (near_own, near_return) in zip(far_parts, near_parts):
        far_arrived = lax.ppermute(far_return, "band", downward)
        near_arrived = lax.ppermute(near_return, "band", downward_one)
        operands += [far_own, near_own, far_arrived, near_arrived]
    width = 16 * grid_size
    spec = pl.BlockSpec((ROWS, width), lambda i: (0, i))
    return pl.pallas_call(
        functools.partial(total_kernel, chunks),
        grid=(cells // width,),
        out_shape=jax.ShapeDtypeStruct((1, slab, cells), F32),
        in_specs=[spec] * len(operands),
        out_specs=pl.BlockSpec((1, slab, width), lambda i: (0, 0, i)),
        compiler_params=pltpu.CompilerParams(vmem_limit_bytes=VMEM_BYTES),
        name="total_terms",
    )(*operands)


def solution(mesh):
    in_specs = (P("band", "fft", None), P("band"))
    out_specs = P("band", "fft", None)
    return jax.shard_map(shards, mesh=mesh, in_specs=in_specs, out_specs=out_specs, check_vma=False)
```

```python
import functools

import jax
import jax.numpy as jnp
import numpy as np
from jax import lax
from jax.experimental import pallas as pl
from jax.experimental.pallas import tpu as pltpu
from jax.sharding import PartitionSpec as P

LANES = 256
CHUNK = 15
ROWS = 16
LEVELS = 32000.0
STEPS_PER_OCTAVE = 64.0
F32 = jnp.float32
BF16 = jnp.bfloat16
VMEM_BYTES = 60 * 1024 * 1024


def round_up(value, multiple):
    return -(-value // multiple) * multiple


def cas_table(grid_size):
    indices = np.arange(grid_size)
    phases = (indices[:, None] * indices[None, :] % grid_size) * (2.0 * np.pi / grid_size)
    return np.cos(phases) + np.sin(phases)


def high_low(table, axis):
    table = table.astype(np.float32)
    high = table.astype(BF16)
    low = (table - high.astype(np.float32)).astype(BF16)
    return jnp.asarray(np.concatenate([high, high, low], axis=axis))


def spread_rows(table, blocks, slab, block_rows):
    spread = np.zeros((blocks * block_rows, table.shape[1]))
    for block in range(blocks):
        spread[block * block_rows : block * block_rows + slab] = table[block * slab : (block + 1) * slab]
    return spread


def spread_planes(table, blocks, slab):
    planes = round_up(slab, CHUNK) // CHUNK * ROWS
    spread = np.zeros((blocks * planes, table.shape[1]))
    for plane in range(blocks * slab):
        block, own = divmod(plane, slab)
        spread[block * planes + own // CHUNK * ROWS + own % CHUNK] = table[plane]
    return spread


def folded_squares(indices, grid_size):
    folded = jnp.minimum(indices, grid_size - indices).astype(F32)
    return folded * folded


def sine_of_half_turns(turns):
    angle = turns * jnp.pi
    square = angle * angle
    series = jnp.full_like(square, 1.0 / 6227020800.0)
    for factor in (-1.0 / 39916800.0, 1.0 / 362880.0, -1.0 / 5040.0, 1.0 / 120.0, -1.0 / 6.0, 1.0):
        series = series * square + factor
    return angle * series


def truncated_kernel(grid_size, slab, rows):
    lanes = folded_squares(jnp.minimum(jnp.arange(LANES, dtype=jnp.int32), grid_size), grid_size)
    folded = jnp.arange(round_up(grid_size // 2 + 1, 8), dtype=jnp.int32).astype(F32)
    squares = folded * folded
    own_rows = lax.axis_index("fft") * slab + jnp.arange(rows, dtype=jnp.int32)
    row_squares = folded_squares(own_rows, grid_size)
    summed = row_squares[:, None, None] + squares[None, :, None] + lanes[None, None, :]
    safe_sum = jnp.maximum(summed, 1.0)
    half_radius = 0.5 * jnp.sqrt(safe_sum)
    sine = sine_of_half_turns(half_radius - jnp.round(half_radius))
    profile = jnp.where(summed > 0.5, 4.0 * sine * sine / (jnp.pi * jnp.pi * safe_sum), 1.0)
    return profile * (0.25 / float(grid_size) ** 1.5)


def parts_of(value):
    high = value.astype(BF16)
    return high, (value - high.astype(F32)).astype(BF16)


def dot(left, right):
    return jnp.dot(left, right, preferred_element_type=F32)


def times_table(value, table):
    high, low = parts_of(value)
    return dot(jnp.concatenate([high, low, high], axis=1), table)


def table_times(table, value):
    high, low = parts_of(value)
    return dot(table, jnp.concatenate([high, low, high], axis=0))


def exponent_of(largest):
    return jnp.ceil(jnp.log2(jnp.maximum(largest, 1e-30)) * STEPS_PER_OCTAVE)


def step_of(exponent):
    return jnp.exp2(exponent * (1.0 / STEPS_PER_OCTAVE))


def coded(value):
    exponent = exponent_of(jnp.max(jnp.abs(value), axis=-2, keepdims=True))
    scaled = jnp.round(value * (LEVELS / step_of(exponent)))
    row = lax.broadcasted_iota(jnp.int32, value.shape, value.ndim - 2)
    return jnp.where(row == CHUNK, exponent, scaled)


def decoded(code):
    return code * (step_of(code[..., CHUNK:, :]) * (1.0 / LEVELS))


def to_wire(code):
    return code.astype(jnp.int32).astype(jnp.int16)


def from_wire(wire):
    return wire.astype(jnp.int32).astype(F32)


def shared_lanes(first, second):
    lane = lax.broadcasted_iota(jnp.int32, first.shape, first.ndim - 1)
    return jnp.where(lane < 64, first, pltpu.roll(second, 64, second.ndim - 1))


def unshared(both):
    lane = lax.broadcasted_iota(jnp.int32, both.shape, both.ndim - 1)
    first = jnp.where(lane < 64, both, 0.0)
    second = jnp.where(lane < 64, pltpu.roll(both, 64, both.ndim - 1), 0.0)
    return first, second


def group_slices(group_lanes, grid_size):
    for row in range(group_lanes // grid_size):
        first, offset = divmod(row * grid_size, 128)
        yield row, first, offset, -(-(offset + grid_size) // 128)


def forward_kernel(blocks, block_rows, a_ref, b_ref, z_ref, y_ref, out_ref, rows_z, rows_y, buf):
    cells = a_ref.shape[1]
    grid_size = rows_z.shape[0]
    half = out_ref.shape[1] // 3
    group_lanes = 8 * grid_size
    z_table, y_table = z_ref[...], y_ref[...]

    @pl.loop(0, cells // group_lanes, unroll=2)
    def _(group):
        lanes = pl.ds(pl.multiple_of(group * group_lanes, 128), group_lanes)
        flat = a_ref[:, lanes].astype(F32) * b_ref[:, lanes].astype(F32)
        for row, first, offset, tiles in group_slices(group_lanes, grid_size):
            window = flat[:, first * 128 : (first + tiles) * 128]
            if offset:
                window = pltpu.roll(window, tiles * 128 - offset, 1)
            rows_z[group * 8 + row] = window[:, :LANES]

    @pl.loop(0, 2)
    def _(part):
        count = grid_size // 2
        at = pl.ds(pl.multiple_of(part * count, 8), count)
        along_z = times_table(rows_z[at].reshape(count * ROWS, LANES), z_table)
        rows_y[:, at, :] = jnp.transpose(along_z.reshape(count, ROWS, LANES), (1, 0, 2))

    @pl.loop(0, 2)
    def _(part):
        along_y = jnp.stack([table_times(y_table, rows_y[part * 8 + i]) for i in range(8)])
        at = pl.ds(pl.multiple_of(part * 8, 8), 8)
        buf[:, at, :] = jnp.transpose(along_y, (1, 0, 2))

    @pl.loop(0, half)
    def _(row):
        for block in range(blocks):
            first = coded(buf[block * block_rows + row])
            second = coded(buf[block * block_rows + half + row])
            out_ref[block, row] = to_wire(first[:, :128])
            out_ref[block, half + row] = to_wire(second[:, :128])
            out_ref[block, 2 * half + row] = to_wire(shared_lanes(first[:, 128:], second[:, 128:]))


def filter_kernel(chunks, *refs):
    in_refs, (w_ref, forward_ref, inverse_ref, out_ref) = refs[:chunks], refs[chunks:]
    blocks, half = out_ref.shape[0], out_ref.shape[1] // 3
    middle = forward_ref.shape[0] // 2
    forward, inverse = forward_ref[...], inverse_ref[...]

    @pl.loop(0, half, unroll=2)
    def _(row):
        upper = [unshared(from_wire(ref[:, 2 * half + row])) for ref in in_refs]
        codes = []
        for i in range(2):
            at = row + i * half
            fields = [
                decoded(jnp.concatenate([from_wire(ref[:, at]), upper[chunk][i]], axis=-1))
                for chunk, ref in enumerate(in_refs)
            ]
            field = jnp.concatenate(fields, axis=1).reshape(blocks * chunks * ROWS, LANES)
            lower_w = w_ref[at, :middle]
            rows = lax.broadcasted_iota(jnp.int32, lower_w.shape, 0)
            upper_w = jnp.where(rows == 0, w_ref[at, middle : middle + 1], lower_w)
            spectrum = table_times(forward, field) * jnp.concatenate([lower_w, upper_w], axis=0)
            filtered = table_times(inverse, spectrum).reshape(blocks, chunks, ROWS, LANES)
            code = coded(filtered).reshape(blocks, chunks * ROWS, LANES)
            out_ref[:, at] = to_wire(code[..., :128])
            codes.append(code[..., 128:])
        out_ref[:, 2 * half + row] = to_wire(shared_lanes(codes[0], codes[1]))


def back_kernel(blocks, block_rows, in_ref, a_ref, b_ref, occ, z_ref, y_ref, own_ref, ret_ref, buf, rows_z, field):
    cells = a_ref.shape[1]
    grid_size = rows_z.shape[0]
    half = in_ref.shape[1] // 3
    group_lanes = 8 * grid_size
    z_table, y_table = z_ref[...], y_ref[...]
    home = -0.5 * occ[0]

    for block in range(blocks):
        base = block * block_rows
        buf[base + 2 * half : base + block_rows] = jnp.zeros((block_rows - 2 * half, ROWS, LANES), F32)

    @pl.loop(0, half)
    def _(row):
        for block in range(blocks):
            base = block * block_rows
            upper = unshared(from_wire(in_ref[block, 2 * half + row]))
            for i in range(2):
                at = row + i * half
                code = jnp.concatenate([from_wire(in_ref[block, at]), upper[i]], axis=-1)
                buf[base + at] = decoded(code)

    @pl.loop(0, 2)
    def _(part):
        rows = pl.ds(pl.multiple_of(part * 8, 8), 8)
        mixed = jnp.transpose(buf[:, rows, :], (1, 0, 2))
        along_y = jnp.stack([table_times(y_table, mixed[i]) for i in range(8)])
        along_z = times_table(along_y.reshape(8 * grid_size, LANES), z_table)
        rows_z[...] = jnp.transpose(along_z.reshape(8, grid_size, LANES), (1, 0, 2))

        @pl.loop(0, cells // group_lanes, unroll=2)
        def _(group):
            tiles_of = [None] * (group_lanes // 128)
            for row, first, offset, tiles in group_slices(group_lanes, grid_size):
                window = rows_z[group * 8 + row]
                if tiles * 128 > LANES:
                    window = jnp.concatenate([window, jnp.zeros((8, tiles * 128 - LANES), F32)], axis=1)
                if offset:
                    window = pltpu.roll(window, offset, 1)
                for tile in range(tiles):
                    piece = window[:, tile * 128 : (tile + 1) * 128]
                    before = tiles_of[first + tile]
                    tiles_of[first + tile] = piece if before is None else before + piece
            lanes = pl.ds(pl.multiple_of(group * group_lanes, 128), group_lanes)
            field[rows, lanes] = jnp.concatenate(tiles_of, axis=1)

    @pl.loop(0, cells // group_lanes)
    def _(group):
        lanes = pl.ds(pl.multiple_of(group * group_lanes, 128), group_lanes)
        potential = field[:, lanes]
        visitor = b_ref[:, lanes].astype(F32)
        own_ref[:, lanes] = potential * visitor * (-0.5 * visitor[CHUNK:])
        terms = potential * a_ref[:, lanes].astype(F32) * home
        ret_ref[:, lanes] = to_wire(coded(terms))


def total_kernel(far_own, near_own, far_arrived, near_arrived, *refs):
    out_ref = refs[-1]
    total = far_own[...] + near_own[...]
    total = total + decoded(from_wire(far_arrived[...])) + decoded(from_wire(near_arrived[...]))
    out_ref[:, 0, :] = total[: out_ref.shape[0]]


def call(kernel, out_shape, scratch, name, flops, operands, in_specs=None):
    single = pl.BlockSpec(memory_space=pltpu.VMEM)
    bytes_moved = sum(o.size * o.dtype.itemsize for o in operands)
    return pl.pallas_call(
        kernel,
        grid=(1,) if in_specs else (),
        out_shape=out_shape,
        in_specs=in_specs or [single] * len(operands),
        out_specs=[single] * len(out_shape) if isinstance(out_shape, list) else single,
        scratch_shapes=scratch,
        compiler_params=pltpu.CompilerParams(vmem_limit_bytes=VMEM_BYTES),
        cost_estimate=pl.CostEstimate(flops=flops, bytes_accessed=bytes_moved, transcendentals=0),
        name=name,
    )(*operands)


def exchange(wire):
    return lax.all_to_all(wire, "fft", split_axis=0, concat_axis=0, tiled=True)


def shards(wavefunctions, band_occ):
    _, slab, cells = wavefunctions.shape
    blocks = lax.axis_size("fft")
    bands = lax.axis_size("band")
    grid_size = slab * blocks
    chunks = round_up(slab, CHUNK) // CHUNK
    planes = chunks * ROWS
    block_rows = round_up(slab, 8)
    half = (slab + 1) // 2
    ky_rows = blocks * block_rows

    table = cas_table(grid_size)
    square_table = np.zeros((LANES, LANES))
    square_table[:grid_size, :grid_size] = table
    to_ky = spread_rows(table, blocks, slab, block_rows)
    middle = grid_size // 2
    kx_order = np.concatenate([np.arange(middle), [middle], grid_size - np.arange(1, middle)])
    to_x = spread_planes(table[:, kx_order], blocks, slab)
    z_table = high_low(square_table, 0)
    y_forward, y_back = high_low(to_ky, 1), high_low(to_ky.T, 1)
    x_forward, x_back = high_low(to_x.T, 1), high_low(to_x, 1)
    profile = truncated_kernel(grid_size, slab, 2 * half)

    occupied = band_occ.astype(BF16)
    upward = [(i, (i + 2) % bands) for i in range(bands)]
    downward = [(i, (i - 2) % bands) for i in range(bands)]
    odd_downward = [pair for pair in downward if pair[0] % 2 == 1]
    even_downward = [pair for pair in downward if pair[0] % 2 == 0]
    downward_one = [(i, (i - 1) % bands) for i in range(bands)]
    swap = [(i, i ^ 1) for i in range(bands)]
    is_odd = lax.axis_index("band") % 2 == 1

    def chunk_of(chunk):
        piece = wavefunctions[0, chunk * CHUNK : (chunk + 1) * CHUNK]
        return jnp.pad(piece, ((0, ROWS - piece.shape[0]), (0, 0)))

    home = [chunk_of(chunk) for chunk in range(chunks)]
    spare_row = jnp.arange(ROWS, dtype=jnp.int32)[:, None] == CHUNK
    carrying = [jnp.where(spare_row, occupied, piece) for piece in home]
    far, near = [], []
    for chunk in range(chunks):
        sent = carrying[chunk]
        if far:
            sent, far[-1] = lax.optimization_barrier((sent, far[-1]))
        far.append(lax.ppermute(sent, "band", upward))
    far[0], profile = lax.optimization_barrier((far[0], profile))
    for chunk in range(chunks):
        near.append(lax.ppermute(jnp.where(is_odd, far[chunk], carrying[chunk]), "band", swap))
    flops = 12 * ROWS * grid_size**3

    def forward(chunk, visitor):
        return call(
            functools.partial(forward_kernel, blocks, block_rows),
            jax.ShapeDtypeStruct((blocks, 3 * half, ROWS, 128), jnp.int16),
            [
                pltpu.VMEM((grid_size, ROWS, LANES), F32),
                pltpu.VMEM((ROWS, grid_size, LANES), F32),
                pltpu.VMEM((ky_rows, ROWS, LANES), F32),
            ],
            "density_to_ky_kz",
            flops,
            [home[chunk], visitor[chunk], z_table, y_forward],
        )

    def filtered(wires):
        return call(
            functools.partial(filter_kernel, chunks),
            jax.ShapeDtypeStruct((blocks, 3 * half, planes, 128), jnp.int16),
            [],
            "filter_along_x",
            chunks * flops,
            [*wires, profile, x_forward, x_back],
        )

    def back(wire, chunk, visitor, factors):
        whole = pl.BlockSpec(memory_space=pltpu.VMEM)
        piece = pl.BlockSpec((blocks, 3 * half, ROWS, 128), lambda i: (0, 0, chunk, 0))
        return call(
            functools.partial(back_kernel, blocks, block_rows),
            [
                jax.ShapeDtypeStruct((ROWS, cells), F32),
                jax.ShapeDtypeStruct((ROWS, cells), jnp.int16),
            ],
            [
                pltpu.VMEM((ky_rows, ROWS, LANES), F32),
                pltpu.VMEM((grid_size, 8, LANES), F32),
                pltpu.VMEM((ROWS, cells), F32),
            ],
            "potential_terms",
            flops,
            [wire, home[chunk], visitor[chunk], factors, z_table, y_back],
            [piece, whole, whole, pl.BlockSpec(memory_space=pltpu.SMEM), whole, whole],
        )

    factors = occupied.astype(F32)

    far_wires = [exchange(forward(chunk, far)) for chunk in range(chunks)]
    near_wires = [exchange(forward(chunk, near)) for chunk in range(chunks)]
    far_wire = exchange(filtered(far_wires))
    near_wire = exchange(filtered(near_wires))
    def returned(chunk, terms):
        route = chunk % 3
        if route == 0:
            crossed = lax.ppermute(terms, "band", swap)
            return jnp.where(is_odd, lax.ppermute(crossed, "band", odd_downward), crossed)
        if route == 1:
            lowered = lax.ppermute(terms, "band", even_downward)
            return lax.ppermute(jnp.where(is_odd, terms, lowered), "band", swap)
        return lax.ppermute(terms, "band", downward_one)

    far_parts, near_parts = [], []
    for wire, visitor, parts in ((far_wire, far, far_parts), (near_wire, near, near_parts)):
        for chunk in range(chunks):
            parts.append(back(wire, chunk, visitor, factors))
            factors, *parts[-1] = lax.optimization_barrier((factors, *parts[-1]))
    width = 16 * grid_size
    spec = pl.BlockSpec((ROWS, width), lambda i: (0, i))
    result = None
    for chunk in range(chunks):
        (far_own, far_return), (near_own, near_return) = far_parts[chunk], near_parts[chunk]
        operands = [far_own, near_own, lax.ppermute(far_return, "band", downward), returned(chunk, near_return)]
        started = [] if result is None else [result]
        result = pl.pallas_call(
            total_kernel,
            grid=(cells // width,),
            out_shape=jax.ShapeDtypeStruct((slab, 1, cells), F32),
            in_specs=[spec] * 4 + [pl.BlockSpec(memory_space=pl.ANY)] * len(started),
            out_specs=pl.BlockSpec((min(CHUNK, slab), 1, width), functools.partial(lambda at, i: (at, 0, i), chunk)),
            input_output_aliases={4: 0} if started else {},
            compiler_params=pltpu.CompilerParams(vmem_limit_bytes=VMEM_BYTES),
            name="total_terms",
        )(*operands, *started)
    return result.reshape(1, slab, cells)


def solution(mesh):
    in_specs = (P("band", "fft", None), P("band"))
    out_specs = P("band", "fft", None)
    return jax.shard_map(shards, mesh=mesh, in_specs=in_specs, out_specs=out_specs, check_vma=False)
```

```python
import functools

import jax
import jax.numpy as jnp
import numpy as np
from jax import lax
from jax.experimental import pallas as pl
from jax.experimental.pallas import tpu as pltpu
from jax.sharding import PartitionSpec as P

LANES = 256
CHUNK = 15
ROWS = 16
LEVELS = 32000.0
STEPS_PER_OCTAVE = 64.0
F32 = jnp.float32
BF16 = jnp.bfloat16
VMEM_BYTES = 60 * 1024 * 1024


def round_up(value, multiple):
    return -(-value // multiple) * multiple


def cas_table(grid_size):
    indices = np.arange(grid_size)
    phases = (indices[:, None] * indices[None, :] % grid_size) * (2.0 * np.pi / grid_size)
    return np.cos(phases) + np.sin(phases)


def high_low(table, axis):
    table = table.astype(np.float32)
    high = table.astype(BF16)
    low = (table - high.astype(np.float32)).astype(BF16)
    return jnp.asarray(np.concatenate([high, high, low], axis=axis))


def spread_rows(table, blocks, slab, block_rows):
    spread = np.zeros((blocks * block_rows, table.shape[1]))
    for block in range(blocks):
        spread[block * block_rows : block * block_rows + slab] = table[block * slab : (block + 1) * slab]
    return spread


def spread_planes(table, blocks, slab):
    planes = round_up(slab, CHUNK) // CHUNK * ROWS
    spread = np.zeros((blocks * planes, table.shape[1]))
    for plane in range(blocks * slab):
        block, own = divmod(plane, slab)
        spread[block * planes + own // CHUNK * ROWS + own % CHUNK] = table[plane]
    return spread


def folded_squares(indices, grid_size):
    folded = jnp.minimum(indices, grid_size - indices).astype(F32)
    return folded * folded


def sine_of_half_turns(turns):
    angle = turns * jnp.pi
    square = angle * angle
    series = jnp.full_like(square, 1.0 / 6227020800.0)
    for factor in (-1.0 / 39916800.0, 1.0 / 362880.0, -1.0 / 5040.0, 1.0 / 120.0, -1.0 / 6.0, 1.0):
        series = series * square + factor
    return angle * series


def truncated_kernel(grid_size, slab, rows):
    lanes = folded_squares(jnp.minimum(jnp.arange(LANES, dtype=jnp.int32), grid_size), grid_size)
    folded = jnp.arange(round_up(grid_size // 2 + 1, 8), dtype=jnp.int32).astype(F32)
    squares = folded * folded
    own_rows = lax.axis_index("fft") * slab + jnp.arange(rows, dtype=jnp.int32)
    row_squares = folded_squares(own_rows, grid_size)
    summed = row_squares[:, None, None] + squares[None, :, None] + lanes[None, None, :]
    safe_sum = jnp.maximum(summed, 1.0)
    half_radius = 0.5 * jnp.sqrt(safe_sum)
    sine = sine_of_half_turns(half_radius - jnp.round(half_radius))
    profile = jnp.where(summed > 0.5, 4.0 * sine * sine / (jnp.pi * jnp.pi * safe_sum), 1.0)
    return profile * (0.25 / float(grid_size) ** 1.5)


def parts_of(value):
    high = value.astype(BF16)
    return high, (value - high.astype(F32)).astype(BF16)


def dot(left, right):
    return jnp.dot(left, right, preferred_element_type=F32)


def times_table(value, table):
    high, low = parts_of(value)
    return dot(jnp.concatenate([high, low, high], axis=1), table)


def table_times(table, value):
    high, low = parts_of(value)
    return dot(table, jnp.concatenate([high, low, high], axis=0))


def exponent_of(largest):
    return jnp.ceil(jnp.log2(jnp.maximum(largest, 1e-30)) * STEPS_PER_OCTAVE)


def step_of(exponent):
    return jnp.exp2(exponent * (1.0 / STEPS_PER_OCTAVE))


def coded(value):
    exponent = exponent_of(jnp.max(jnp.abs(value), axis=-2, keepdims=True))
    scaled = jnp.round(value * (LEVELS / step_of(exponent)))
    row = lax.broadcasted_iota(jnp.int32, value.shape, value.ndim - 2)
    return jnp.where(row == CHUNK, exponent, scaled)


def decoded(code):
    return code * (step_of(code[..., CHUNK:, :]) * (1.0 / LEVELS))


def to_wire(code):
    return code.astype(jnp.int32).astype(jnp.int16)


def from_wire(wire):
    return wire.astype(jnp.int32).astype(F32)


def shared_lanes(first, second):
    lane = lax.broadcasted_iota(jnp.int32, first.shape, first.ndim - 1)
    return jnp.where(lane < 64, first, pltpu.roll(second, 64, second.ndim - 1))


def unshared(both):
    lane = lax.broadcasted_iota(jnp.int32, both.shape, both.ndim - 1)
    first = jnp.where(lane < 64, both, 0.0)
    second = jnp.where(lane < 64, pltpu.roll(both, 64, both.ndim - 1), 0.0)
    return first, second


def group_slices(group_lanes, grid_size):
    for row in range(group_lanes // grid_size):
        first, offset = divmod(row * grid_size, 128)
        yield row, first, offset, -(-(offset + grid_size) // 128)


def forward_kernel(blocks, block_rows, a_ref, b_ref, z_ref, y_ref, out_ref, rows_z, rows_y, buf):
    cells = a_ref.shape[1]
    grid_size = rows_z.shape[0]
    half = out_ref.shape[1] // 3
    group_lanes = 8 * grid_size
    z_table, y_table = z_ref[...], y_ref[...]

    @pl.loop(0, cells // group_lanes, unroll=2)
    def _(group):
        lanes = pl.ds(pl.multiple_of(group * group_lanes, 128), group_lanes)
        flat = a_ref[:, lanes].astype(F32) * b_ref[:, lanes].astype(F32)
        for row, first, offset, tiles in group_slices(group_lanes, grid_size):
            window = flat[:, first * 128 : (first + tiles) * 128]
            if offset:
                window = pltpu.roll(window, tiles * 128 - offset, 1)
            rows_z[group * 8 + row] = window[:, :LANES]

    @pl.loop(0, 2)
    def _(part):
        count = grid_size // 2
        at = pl.ds(pl.multiple_of(part * count, 8), count)
        along_z = times_table(rows_z[at].reshape(count * ROWS, LANES), z_table)
        rows_y[:, at, :] = jnp.transpose(along_z.reshape(count, ROWS, LANES), (1, 0, 2))

    @pl.loop(0, 2)
    def _(part):
        along_y = jnp.stack([table_times(y_table, rows_y[part * 8 + i]) for i in range(8)])
        at = pl.ds(pl.multiple_of(part * 8, 8), 8)
        buf[:, at, :] = jnp.transpose(along_y, (1, 0, 2))

    @pl.loop(0, half)
    def _(row):
        for block in range(blocks):
            first = coded(buf[block * block_rows + row])
            second = coded(buf[block * block_rows + half + row])
            out_ref[block, row] = to_wire(first[:, :128])
            out_ref[block, half + row] = to_wire(second[:, :128])
            out_ref[block, 2 * half + row] = to_wire(shared_lanes(first[:, 128:], second[:, 128:]))


def filter_kernel(chunks, *refs):
    in_refs, (w_ref, forward_ref, inverse_ref, out_ref) = refs[:chunks], refs[chunks:]
    blocks, half = out_ref.shape[0], out_ref.shape[1] // 3
    middle = forward_ref.shape[0] // 2
    forward, inverse = forward_ref[...], inverse_ref[...]

    @pl.loop(0, half, unroll=2)
    def _(row):
        upper = [unshared(from_wire(ref[:, 2 * half + row])) for ref in in_refs]
        codes = []
        for i in range(2):
            at = row + i * half
            fields = [
                decoded(jnp.concatenate([from_wire(ref[:, at]), upper[chunk][i]], axis=-1))
                for chunk, ref in enumerate(in_refs)
            ]
            field = jnp.concatenate(fields, axis=1).reshape(blocks * chunks * ROWS, LANES)
            lower_w = w_ref[at, :middle]
            rows = lax.broadcasted_iota(jnp.int32, lower_w.shape, 0)
            upper_w = jnp.where(rows == 0, w_ref[at, middle : middle + 1], lower_w)
            spectrum = table_times(forward, field) * jnp.concatenate([lower_w, upper_w], axis=0)
            filtered = table_times(inverse, spectrum).reshape(blocks, chunks, ROWS, LANES)
            code = coded(filtered).reshape(blocks, chunks * ROWS, LANES)
            out_ref[:, at] = to_wire(code[..., :128])
            codes.append(code[..., 128:])
        out_ref[:, 2 * half + row] = to_wire(shared_lanes(codes[0], codes[1]))


def back_kernel(blocks, block_rows, in_ref, a_ref, b_ref, occ, z_ref, y_ref, own_ref, ret_ref, buf, rows_z, field):
    cells = a_ref.shape[1]
    grid_size = rows_z.shape[0]
    half = in_ref.shape[1] // 3
    group_lanes = 8 * grid_size
    z_table, y_table = z_ref[...], y_ref[...]
    home = -0.5 * occ[0]

    for block in range(blocks):
        base = block * block_rows
        buf[base + 2 * half : base + block_rows] = jnp.zeros((block_rows - 2 * half, ROWS, LANES), F32)

    @pl.loop(0, half)
    def _(row):
        for block in range(blocks):
            base = block * block_rows
            upper = unshared(from_wire(in_ref[block, 2 * half + row]))
            for i in range(2):
                at = row + i * half
                code = jnp.concatenate([from_wire(in_ref[block, at]), upper[i]], axis=-1)
                buf[base + at] = decoded(code)

    @pl.loop(0, 2)
    def _(part):
        rows = pl.ds(pl.multiple_of(part * 8, 8), 8)
        mixed = jnp.transpose(buf[:, rows, :], (1, 0, 2))
        along_y = jnp.stack([table_times(y_table, mixed[i]) for i in range(8)])
        along_z = times_table(along_y.reshape(8 * grid_size, LANES), z_table)
        rows_z[...] = jnp.transpose(along_z.reshape(8, grid_size, LANES), (1, 0, 2))

        @pl.loop(0, cells // group_lanes, unroll=2)
        def _(group):
            tiles_of = [None] * (group_lanes // 128)
            for row, first, offset, tiles in group_slices(group_lanes, grid_size):
                window = rows_z[group * 8 + row]
                if tiles * 128 > LANES:
                    window = jnp.concatenate([window, jnp.zeros((8, tiles * 128 - LANES), F32)], axis=1)
                if offset:
                    window = pltpu.roll(window, offset, 1)
                for tile in range(tiles):
                    piece = window[:, tile * 128 : (tile + 1) * 128]
                    before = tiles_of[first + tile]
                    tiles_of[first + tile] = piece if before is None else before + piece
            lanes = pl.ds(pl.multiple_of(group * group_lanes, 128), group_lanes)
            field[rows, lanes] = jnp.concatenate(tiles_of, axis=1)

    @pl.loop(0, cells // group_lanes)
    def _(group):
        lanes = pl.ds(pl.multiple_of(group * group_lanes, 128), group_lanes)
        potential = field[:, lanes]
        visitor = b_ref[:, lanes].astype(F32)
        own_ref[:, lanes] = potential * visitor * (-0.5 * visitor[CHUNK:])
        terms = potential * a_ref[:, lanes].astype(F32) * home
        ret_ref[:, lanes] = to_wire(coded(terms))


def total_kernel(far_own, near_own, far_arrived, near_arrived, *refs):
    out_ref = refs[-1]
    total = far_own[...] + near_own[...]
    total = total + decoded(from_wire(far_arrived[...])) + decoded(from_wire(near_arrived[...]))
    out_ref[:, 0, :] = total[: out_ref.shape[0]]


def call(kernel, out_shape, scratch, name, flops, operands, in_specs=None):
    single = pl.BlockSpec(memory_space=pltpu.VMEM)
    bytes_moved = sum(o.size * o.dtype.itemsize for o in operands)
    return pl.pallas_call(
        kernel,
        grid=(1,) if in_specs else (),
        out_shape=out_shape,
        in_specs=in_specs or [single] * len(operands),
        out_specs=[single] * len(out_shape) if isinstance(out_shape, list) else single,
        scratch_shapes=scratch,
        compiler_params=pltpu.CompilerParams(vmem_limit_bytes=VMEM_BYTES),
        cost_estimate=pl.CostEstimate(flops=flops, bytes_accessed=bytes_moved, transcendentals=0),
        name=name,
    )(*operands)


def exchange(wire):
    return lax.all_to_all(wire, "fft", split_axis=0, concat_axis=0, tiled=True)


def shards(wavefunctions, band_occ):
    _, slab, cells = wavefunctions.shape
    blocks = lax.axis_size("fft")
    bands = lax.axis_size("band")
    grid_size = slab * blocks
    chunks = round_up(slab, CHUNK) // CHUNK
    planes = chunks * ROWS
    block_rows = round_up(slab, 8)
    half = (slab + 1) // 2
    ky_rows = blocks * block_rows

    table = cas_table(grid_size)
    square_table = np.zeros((LANES, LANES))
    square_table[:grid_size, :grid_size] = table
    to_ky = spread_rows(table, blocks, slab, block_rows)
    middle = grid_size // 2
    kx_order = np.concatenate([np.arange(middle), [middle], grid_size - np.arange(1, middle)])
    to_x = spread_planes(table[:, kx_order], blocks, slab)
    z_table = high_low(square_table, 0)
    y_forward, y_back = high_low(to_ky, 1), high_low(to_ky.T, 1)
    x_forward, x_back = high_low(to_x.T, 1), high_low(to_x, 1)
    profile = truncated_kernel(grid_size, slab, 2 * half)

    occupied = band_occ.astype(BF16)
    upward = [(i, (i + 2) % bands) for i in range(bands)]
    downward = [(i, (i - 2) % bands) for i in range(bands)]
    odd_downward = [pair for pair in downward if pair[0] % 2 == 1]
    even_downward = [pair for pair in downward if pair[0] % 2 == 0]
    downward_one = [(i, (i - 1) % bands) for i in range(bands)]
    swap = [(i, i ^ 1) for i in range(bands)]
    is_odd = lax.axis_index("band") % 2 == 1

    def chunk_of(chunk):
        piece = wavefunctions[0, chunk * CHUNK : (chunk + 1) * CHUNK]
        return jnp.pad(piece, ((0, ROWS - piece.shape[0]), (0, 0)))

    home = [chunk_of(chunk) for chunk in range(chunks)]
    spare_row = jnp.arange(ROWS, dtype=jnp.int32)[:, None] == CHUNK
    carrying = [jnp.where(spare_row, occupied, piece) for piece in home]
    far, near = [], []
    for chunk in range(chunks):
        sent = carrying[chunk]
        if chunk >= 2:
            sent, far[chunk - 2] = lax.optimization_barrier((sent, far[chunk - 2]))
        far.append(lax.ppermute(sent, "band", upward))
    far[0], profile = lax.optimization_barrier((far[0], profile))
    for chunk in range(chunks):
        near.append(lax.ppermute(jnp.where(is_odd, far[chunk], carrying[chunk]), "band", swap))
    flops = 12 * ROWS * grid_size**3

    def forward(chunk, visitor):
        return call(
            functools.partial(forward_kernel, blocks, block_rows),
            jax.ShapeDtypeStruct((blocks, 3 * half, ROWS, 128), jnp.int16),
            [
                pltpu.VMEM((grid_size, ROWS, LANES), F32),
                pltpu.VMEM((ROWS, grid_size, LANES), F32),
                pltpu.VMEM((ky_rows, ROWS, LANES), F32),
            ],
            "density_to_ky_kz",
            flops,
            [home[chunk], visitor[chunk], z_table, y_forward],
        )

    def filtered(wires):
        return call(
            functools.partial(filter_kernel, chunks),
            jax.ShapeDtypeStruct((blocks, 3 * half, planes, 128), jnp.int16),
            [],
            "filter_along_x",
            chunks * flops,
            [*wires, profile, x_forward, x_back],
        )

    def back(wire, chunk, visitor, factors):
        whole = pl.BlockSpec(memory_space=pltpu.VMEM)
        piece = pl.BlockSpec((blocks, 3 * half, ROWS, 128), lambda i: (0, 0, chunk, 0))
        return call(
            functools.partial(back_kernel, blocks, block_rows),
            [
                jax.ShapeDtypeStruct((ROWS, cells), F32),
                jax.ShapeDtypeStruct((ROWS, cells), jnp.int16),
            ],
            [
                pltpu.VMEM((ky_rows, ROWS, LANES), F32),
                pltpu.VMEM((grid_size, 8, LANES), F32),
                pltpu.VMEM((ROWS, cells), F32),
            ],
            "potential_terms",
            flops,
            [wire, home[chunk], visitor[chunk], factors, z_table, y_back],
            [piece, whole, whole, pl.BlockSpec(memory_space=pltpu.SMEM), whole, whole],
        )

    factors = occupied.astype(F32)

    far_wires = [exchange(forward(chunk, far)) for chunk in range(chunks)]
    near_wires = [exchange(forward(chunk, near)) for chunk in range(chunks)]
    far_wire = exchange(filtered(far_wires))
    near_wire = exchange(filtered(near_wires))
    def returned(chunk, terms):
        route = chunk % 3
        if route == 0:
            crossed = lax.ppermute(terms, "band", swap)
            crossed, far_arrived[-1] = lax.optimization_barrier((crossed, far_arrived[-1]))
            return jnp.where(is_odd, lax.ppermute(crossed, "band", odd_downward), crossed)
        if route == 1:
            lowered = lax.ppermute(terms, "band", even_downward)
            return lax.ppermute(jnp.where(is_odd, terms, lowered), "band", swap)
        return lax.ppermute(terms, "band", downward_one)

    far_parts, near_parts, far_arrived = [], [], []
    for chunk in range(chunks):
        own, terms = back(far_wire, chunk, far, factors)
        factors, terms = lax.optimization_barrier((factors, terms))
        far_parts.append(own)
        far_arrived.append(lax.ppermute(terms, "band", downward))
    for chunk in range(chunks):
        if chunk >= 1:
            factors, far_arrived[chunk - 1] = lax.optimization_barrier((factors, far_arrived[chunk - 1]))
        own, terms = back(near_wire, chunk, near, factors)
        factors, terms = lax.optimization_barrier((factors, terms))
        near_parts.append((own, terms))
    width = 16 * grid_size
    spec = pl.BlockSpec((ROWS, width), lambda i: (0, i))
    result = None
    for chunk in range(chunks):
        near_own, near_return = near_parts[chunk]
        operands = [far_parts[chunk], near_own, far_arrived[chunk], returned(chunk, near_return)]
        started = [] if result is None else [result]
        result = pl.pallas_call(
            total_kernel,
            grid=(cells // width,),
            out_shape=jax.ShapeDtypeStruct((slab, 1, cells), F32),
            in_specs=[spec] * 4 + [pl.BlockSpec(memory_space=pl.ANY)] * len(started),
            out_specs=pl.BlockSpec((min(CHUNK, slab), 1, width), functools.partial(lambda at, i: (at, 0, i), chunk)),
            input_output_aliases={4: 0} if started else {},
            compiler_params=pltpu.CompilerParams(vmem_limit_bytes=VMEM_BYTES),
            name="total_terms",
        )(*operands, *started)
    return result.reshape(1, slab, cells)


def solution(mesh):
    in_specs = (P("band", "fft", None), P("band"))
    out_specs = P("band", "fft", None)
    return jax.shard_map(shards, mesh=mesh, in_specs=in_specs, out_specs=out_specs, check_vma=False)
```

```python
import functools

import jax
import jax.numpy as jnp
import numpy as np
from jax import lax
from jax.experimental import pallas as pl
from jax.experimental.pallas import tpu as pltpu
from jax.sharding import PartitionSpec as P

LANES = 256
CHUNK = 15
ROWS = 16
LEVELS = 32000.0
STEPS_PER_OCTAVE = 64.0
F32 = jnp.float32
BF16 = jnp.bfloat16
VMEM_BYTES = 60 * 1024 * 1024


def round_up(value, multiple):
    return -(-value // multiple) * multiple


def cas_table(grid_size):
    indices = np.arange(grid_size)
    phases = (indices[:, None] * indices[None, :] % grid_size) * (2.0 * np.pi / grid_size)
    return np.cos(phases) + np.sin(phases)


def high_low(table, axis):
    table = table.astype(np.float32)
    high = table.astype(BF16)
    low = (table - high.astype(np.float32)).astype(BF16)
    return jnp.asarray(np.concatenate([high, high, low], axis=axis))


def spread_rows(table, blocks, slab, block_rows):
    spread = np.zeros((blocks * block_rows, table.shape[1]))
    for block in range(blocks):
        spread[block * block_rows : block * block_rows + slab] = table[block * slab : (block + 1) * slab]
    return spread


def spread_planes(table, blocks, slab):
    planes = round_up(slab, CHUNK) // CHUNK * ROWS
    spread = np.zeros((blocks * planes, table.shape[1]))
    for plane in range(blocks * slab):
        block, own = divmod(plane, slab)
        spread[block * planes + own // CHUNK * ROWS + own % CHUNK] = table[plane]
    return spread


def folded_squares(indices, grid_size):
    folded = jnp.minimum(indices, grid_size - indices).astype(F32)
    return folded * folded


def sine_of_half_turns(turns):
    angle = turns * jnp.pi
    square = angle * angle
    series = jnp.full_like(square, 1.0 / 6227020800.0)
    for factor in (-1.0 / 39916800.0, 1.0 / 362880.0, -1.0 / 5040.0, 1.0 / 120.0, -1.0 / 6.0, 1.0):
        series = series * square + factor
    return angle * series


def truncated_kernel(grid_size, slab, rows):
    lanes = folded_squares(jnp.minimum(jnp.arange(LANES, dtype=jnp.int32), grid_size), grid_size)
    folded = jnp.arange(round_up(grid_size // 2 + 1, 8), dtype=jnp.int32).astype(F32)
    squares = folded * folded
    own_rows = lax.axis_index("fft") * slab + jnp.arange(rows, dtype=jnp.int32)
    row_squares = folded_squares(own_rows, grid_size)
    summed = row_squares[:, None, None] + squares[None, :, None] + lanes[None, None, :]
    safe_sum = jnp.maximum(summed, 1.0)
    half_radius = 0.5 * jnp.sqrt(safe_sum)
    sine = sine_of_half_turns(half_radius - jnp.round(half_radius))
    profile = jnp.where(summed > 0.5, 4.0 * sine * sine / (jnp.pi * jnp.pi * safe_sum), 1.0)
    return profile * (0.25 / float(grid_size) ** 1.5)


def parts_of(value):
    high = value.astype(BF16)
    return high, (value - high.astype(F32)).astype(BF16)


def dot(left, right):
    return jnp.dot(left, right, preferred_element_type=F32)


def times_table(value, table):
    high, low = parts_of(value)
    return dot(jnp.concatenate([high, low, high], axis=1), table)


def table_times(table, value):
    high, low = parts_of(value)
    return dot(table, jnp.concatenate([high, low, high], axis=0))


def exponent_of(largest):
    return jnp.ceil(jnp.log2(jnp.maximum(largest, 1e-30)) * STEPS_PER_OCTAVE)


def step_of(exponent):
    return jnp.exp2(exponent * (1.0 / STEPS_PER_OCTAVE))


def coded(value):
    exponent = exponent_of(jnp.max(jnp.abs(value), axis=-2, keepdims=True))
    scaled = jnp.round(value * (LEVELS / step_of(exponent)))
    row = lax.broadcasted_iota(jnp.int32, value.shape, value.ndim - 2)
    return jnp.where(row == CHUNK, exponent, scaled)


def decoded(code):
    return code * (step_of(code[..., CHUNK:, :]) * (1.0 / LEVELS))


def to_wire(code):
    return code.astype(jnp.int32).astype(jnp.int16)


def from_wire(wire):
    return wire.astype(jnp.int32).astype(F32)


def shared_lanes(first, second):
    lane = lax.broadcasted_iota(jnp.int32, first.shape, first.ndim - 1)
    return jnp.where(lane < 64, first, pltpu.roll(second, 64, second.ndim - 1))


def unshared(both):
    lane = lax.broadcasted_iota(jnp.int32, both.shape, both.ndim - 1)
    first = jnp.where(lane < 64, both, 0.0)
    second = jnp.where(lane < 64, pltpu.roll(both, 64, both.ndim - 1), 0.0)
    return first, second


def group_slices(group_lanes, grid_size):
    for row in range(group_lanes // grid_size):
        first, offset = divmod(row * grid_size, 128)
        yield row, first, offset, -(-(offset + grid_size) // 128)


def forward_kernel(blocks, block_rows, a_ref, b_ref, z_ref, y_ref, out_ref, rows_z, rows_y, buf):
    cells = a_ref.shape[1]
    grid_size = rows_z.shape[0]
    half = out_ref.shape[1] // 3
    group_lanes = 8 * grid_size
    z_table, y_table = z_ref[...], y_ref[...]

    @pl.loop(0, cells // group_lanes, unroll=2)
    def _(group):
        lanes = pl.ds(pl.multiple_of(group * group_lanes, 128), group_lanes)
        flat = a_ref[:, lanes].astype(F32) * b_ref[:, lanes].astype(F32)
        for row, first, offset, tiles in group_slices(group_lanes, grid_size):
            window = flat[:, first * 128 : (first + tiles) * 128]
            if offset:
                window = pltpu.roll(window, tiles * 128 - offset, 1)
            rows_z[group * 8 + row] = window[:, :LANES]

    @pl.loop(0, 2)
    def _(part):
        count = grid_size // 2
        at = pl.ds(pl.multiple_of(part * count, 8), count)
        along_z = times_table(rows_z[at].reshape(count * ROWS, LANES), z_table)
        rows_y[:, at, :] = jnp.transpose(along_z.reshape(count, ROWS, LANES), (1, 0, 2))

    @pl.loop(0, 2)
    def _(part):
        along_y = jnp.stack([table_times(y_table, rows_y[part * 8 + i]) for i in range(8)])
        at = pl.ds(pl.multiple_of(part * 8, 8), 8)
        buf[:, at, :] = jnp.transpose(along_y, (1, 0, 2))

    @pl.loop(0, half)
    def _(row):
        for block in range(blocks):
            first = coded(buf[block * block_rows + row])
            second = coded(buf[block * block_rows + half + row])
            out_ref[block, row] = to_wire(first[:, :128])
            out_ref[block, half + row] = to_wire(second[:, :128])
            out_ref[block, 2 * half + row] = to_wire(shared_lanes(first[:, 128:], second[:, 128:]))


def filter_kernel(chunks, *refs):
    in_refs, (w_ref, forward_ref, inverse_ref, out_ref) = refs[:chunks], refs[chunks:]
    blocks, half = out_ref.shape[0], out_ref.shape[1] // 3
    middle = forward_ref.shape[0] // 2
    forward, inverse = forward_ref[...], inverse_ref[...]

    @pl.loop(0, half, unroll=2)
    def _(row):
        upper = [unshared(from_wire(ref[:, 2 * half + row])) for ref in in_refs]
        codes = []
        for i in range(2):
            at = row + i * half
            fields = [
                decoded(jnp.concatenate([from_wire(ref[:, at]), upper[chunk][i]], axis=-1))
                for chunk, ref in enumerate(in_refs)
            ]
            field = jnp.concatenate(fields, axis=1).reshape(blocks * chunks * ROWS, LANES)
            lower_w = w_ref[at, :middle]
            rows = lax.broadcasted_iota(jnp.int32, lower_w.shape, 0)
            upper_w = jnp.where(rows == 0, w_ref[at, middle : middle + 1], lower_w)
            spectrum = table_times(forward, field) * jnp.concatenate([lower_w, upper_w], axis=0)
            filtered = table_times(inverse, spectrum).reshape(blocks, chunks, ROWS, LANES)
            code = coded(filtered).reshape(blocks, chunks * ROWS, LANES)
            out_ref[:, at] = to_wire(code[..., :128])
            codes.append(code[..., 128:])
        out_ref[:, 2 * half + row] = to_wire(shared_lanes(codes[0], codes[1]))


def back_kernel(blocks, block_rows, adding, in_ref, a_ref, b_ref, occ, z_ref, y_ref, *refs):
    own_ref, ret_ref, buf, rows_z, field = refs[adding:]
    cells = a_ref.shape[1]
    grid_size = rows_z.shape[0]
    half = in_ref.shape[1] // 3
    group_lanes = 8 * grid_size
    z_table, y_table = z_ref[...], y_ref[...]
    home = -0.5 * occ[0]

    for block in range(blocks):
        base = block * block_rows
        buf[base + 2 * half : base + block_rows] = jnp.zeros((block_rows - 2 * half, ROWS, LANES), F32)

    @pl.loop(0, half)
    def _(row):
        for block in range(blocks):
            base = block * block_rows
            upper = unshared(from_wire(in_ref[block, 2 * half + row]))
            for i in range(2):
                at = row + i * half
                code = jnp.concatenate([from_wire(in_ref[block, at]), upper[i]], axis=-1)
                buf[base + at] = decoded(code)

    @pl.loop(0, 2)
    def _(part):
        rows = pl.ds(pl.multiple_of(part * 8, 8), 8)
        mixed = jnp.transpose(buf[:, rows, :], (1, 0, 2))
        along_y = jnp.stack([table_times(y_table, mixed[i]) for i in range(8)])
        along_z = times_table(along_y.reshape(8 * grid_size, LANES), z_table)
        rows_z[...] = jnp.transpose(along_z.reshape(8, grid_size, LANES), (1, 0, 2))

        @pl.loop(0, cells // group_lanes, unroll=2)
        def _(group):
            tiles_of = [None] * (group_lanes // 128)
            for row, first, offset, tiles in group_slices(group_lanes, grid_size):
                window = rows_z[group * 8 + row]
                if tiles * 128 > LANES:
                    window = jnp.concatenate([window, jnp.zeros((8, tiles * 128 - LANES), F32)], axis=1)
                if offset:
                    window = pltpu.roll(window, offset, 1)
                for tile in range(tiles):
                    piece = window[:, tile * 128 : (tile + 1) * 128]
                    before = tiles_of[first + tile]
                    tiles_of[first + tile] = piece if before is None else before + piece
            lanes = pl.ds(pl.multiple_of(group * group_lanes, 128), group_lanes)
            field[rows, lanes] = jnp.concatenate(tiles_of, axis=1)

    @pl.loop(0, cells // group_lanes)
    def _(group):
        lanes = pl.ds(pl.multiple_of(group * group_lanes, 128), group_lanes)
        potential = field[:, lanes]
        visitor = b_ref[:, lanes].astype(F32)
        own_ref[:, lanes] = potential * visitor * (-0.5 * visitor[CHUNK:])
        terms = potential * a_ref[:, lanes].astype(F32) * home
        if adding:
            terms = terms + decoded(from_wire(refs[0][:, lanes])) * occ[1]
        ret_ref[:, lanes] = to_wire(coded(terms))


def total_kernel(far_own, near_own, far_arrived, near_arrived, flags, *refs):
    out_ref = refs[-1]
    total = far_own[...] + near_own[...]
    total = total + decoded(from_wire(far_arrived[...])) + decoded(from_wire(near_arrived[...])) * flags[2]
    out_ref[:, 0, :] = total[: out_ref.shape[0]]


def call(kernel, out_shape, scratch, name, flops, operands, in_specs=None):
    single = pl.BlockSpec(memory_space=pltpu.VMEM)
    bytes_moved = sum(o.size * o.dtype.itemsize for o in operands)
    return pl.pallas_call(
        kernel,
        grid=(1,) if in_specs else (),
        out_shape=out_shape,
        in_specs=in_specs or [single] * len(operands),
        out_specs=[single] * len(out_shape) if isinstance(out_shape, list) else single,
        scratch_shapes=scratch,
        compiler_params=pltpu.CompilerParams(vmem_limit_bytes=VMEM_BYTES),
        cost_estimate=pl.CostEstimate(flops=flops, bytes_accessed=bytes_moved, transcendentals=0),
        name=name,
    )(*operands)


def exchange(wire):
    return lax.all_to_all(wire, "fft", split_axis=0, concat_axis=0, tiled=True)


def shards(wavefunctions, band_occ):
    _, slab, cells = wavefunctions.shape
    blocks = lax.axis_size("fft")
    bands = lax.axis_size("band")
    grid_size = slab * blocks
    chunks = round_up(slab, CHUNK) // CHUNK
    planes = chunks * ROWS
    block_rows = round_up(slab, 8)
    half = (slab + 1) // 2
    ky_rows = blocks * block_rows

    table = cas_table(grid_size)
    square_table = np.zeros((LANES, LANES))
    square_table[:grid_size, :grid_size] = table
    to_ky = spread_rows(table, blocks, slab, block_rows)
    middle = grid_size // 2
    kx_order = np.concatenate([np.arange(middle), [middle], grid_size - np.arange(1, middle)])
    to_x = spread_planes(table[:, kx_order], blocks, slab)
    z_table = high_low(square_table, 0)
    y_forward, y_back = high_low(to_ky, 1), high_low(to_ky.T, 1)
    x_forward, x_back = high_low(to_x.T, 1), high_low(to_x, 1)
    profile = truncated_kernel(grid_size, slab, 2 * half)

    occupied = band_occ.astype(BF16)
    upward = [(i, (i + 2) % bands) for i in range(bands)]
    downward = [(i, (i - 2) % bands) for i in range(bands)]
    swap = [(i, i ^ 1) for i in range(bands)]
    is_odd = lax.axis_index("band") % 2 == 1

    def chunk_of(chunk):
        piece = wavefunctions[0, chunk * CHUNK : (chunk + 1) * CHUNK]
        return jnp.pad(piece, ((0, ROWS - piece.shape[0]), (0, 0)))

    home = [chunk_of(chunk) for chunk in range(chunks)]
    spare_row = jnp.arange(ROWS, dtype=jnp.int32)[:, None] == CHUNK
    carrying = [jnp.where(spare_row, occupied, piece) for piece in home]
    far, near = [], []
    for chunk in range(chunks):
        sent = carrying[chunk]
        far.append(lax.ppermute(sent, "band", upward))
    far[0], profile = lax.optimization_barrier((far[0], profile))
    for chunk in range(chunks):
        near.append(lax.ppermute(jnp.where(is_odd, far[chunk], carrying[chunk]), "band", swap))
    flops = 12 * ROWS * grid_size**3

    def forward(chunk, visitor):
        return call(
            functools.partial(forward_kernel, blocks, block_rows),
            jax.ShapeDtypeStruct((blocks, 3 * half, ROWS, 128), jnp.int16),
            [
                pltpu.VMEM((grid_size, ROWS, LANES), F32),
                pltpu.VMEM((ROWS, grid_size, LANES), F32),
                pltpu.VMEM((ky_rows, ROWS, LANES), F32),
            ],
            "density_to_ky_kz",
            flops,
            [home[chunk], visitor[chunk], z_table, y_forward],
        )

    def filtered(wires):
        return call(
            functools.partial(filter_kernel, chunks),
            jax.ShapeDtypeStruct((blocks, 3 * half, planes, 128), jnp.int16),
            [],
            "filter_along_x",
            chunks * flops,
            [*wires, profile, x_forward, x_back],
        )

    def back(wire, chunk, visitor, factors, added=()):
        whole = pl.BlockSpec(memory_space=pltpu.VMEM)
        piece = pl.BlockSpec((blocks, 3 * half, ROWS, 128), lambda i: (0, 0, chunk, 0))
        return call(
            functools.partial(back_kernel, blocks, block_rows, len(added)),
            [
                jax.ShapeDtypeStruct((ROWS, cells), F32),
                jax.ShapeDtypeStruct((ROWS, cells), jnp.int16),
            ],
            [
                pltpu.VMEM((ky_rows, ROWS, LANES), F32),
                pltpu.VMEM((grid_size, 8, LANES), F32),
                pltpu.VMEM((ROWS, cells), F32),
            ],
            "potential_terms",
            flops,
            [wire, home[chunk], visitor[chunk], factors, z_table, y_back, *added],
            [piece, whole, whole, pl.BlockSpec(memory_space=pltpu.SMEM)] + [whole] * (2 + len(added)),
        )

    odd = is_odd.astype(F32)
    factors = flags = jnp.stack([occupied.astype(F32)[0], odd, 1.0 - odd])

    far_wires = [exchange(forward(chunk, far)) for chunk in range(chunks)]
    near_wires = [exchange(forward(chunk, near)) for chunk in range(chunks)]
    near_wire = exchange(filtered(near_wires))
    far_wire = exchange(filtered(far_wires))
    near_own, crossed, far_own, arrived = [], [], [], []
    for chunk in range(chunks):
        own, terms = back(near_wire, chunk, near, factors)
        factors, terms = lax.optimization_barrier((factors, terms))
        near_own.append(own)
        crossed.append(lax.ppermute(terms, "band", swap))
    for chunk in range(chunks):
        own, terms = back(far_wire, chunk, far, factors, [crossed[chunk]])
        factors, terms = lax.optimization_barrier((factors, terms))
        far_own.append(own)
        arrived.append(lax.ppermute(terms, "band", downward))
    width = 16 * grid_size
    spec = pl.BlockSpec((ROWS, width), lambda i: (0, i))
    result = None
    for chunk in range(chunks):
        operands = [far_own[chunk], near_own[chunk], arrived[chunk], crossed[chunk], flags]
        started = [] if result is None else [result]
        result = pl.pallas_call(
            total_kernel,
            grid=(cells // width,),
            out_shape=jax.ShapeDtypeStruct((slab, 1, cells), F32),
            in_specs=[spec] * 4 + [pl.BlockSpec(memory_space=pltpu.SMEM)] + [pl.BlockSpec(memory_space=pl.ANY)] * len(started),
            out_specs=pl.BlockSpec((min(CHUNK, slab), 1, width), functools.partial(lambda at, i: (at, 0, i), chunk)),
            input_output_aliases={5: 0} if started else {},
            compiler_params=pltpu.CompilerParams(vmem_limit_bytes=VMEM_BYTES),
            name="total_terms",
        )(*operands, *started)
    return result.reshape(1, slab, cells)


def solution(mesh):
    in_specs = (P("band", "fft", None), P("band"))
    out_specs = P("band", "fft", None)
    return jax.shard_map(shards, mesh=mesh, in_specs=in_specs, out_specs=out_specs, check_vma=False)
```

```python
import functools

import jax
import jax.numpy as jnp
import numpy as np
from jax import lax
from jax.experimental import pallas as pl
from jax.experimental.pallas import tpu as pltpu
from jax.sharding import PartitionSpec as P

LANES = 256
CHUNK = 15
ROWS = 16
LEVELS = 32000.0
STEPS_PER_OCTAVE = 64.0
F32 = jnp.float32
BF16 = jnp.bfloat16
VMEM_BYTES = 60 * 1024 * 1024


def round_up(value, multiple):
    return -(-value // multiple) * multiple


def cas_table(grid_size):
    indices = np.arange(grid_size)
    phases = (indices[:, None] * indices[None, :] % grid_size) * (2.0 * np.pi / grid_size)
    return np.cos(phases) + np.sin(phases)


def high_low(table, axis):
    table = table.astype(np.float32)
    high = table.astype(BF16)
    low = (table - high.astype(np.float32)).astype(BF16)
    return jnp.asarray(np.concatenate([high, high, low], axis=axis))


def spread_rows(table, blocks, slab, block_rows):
    spread = np.zeros((blocks * block_rows, table.shape[1]))
    for block in range(blocks):
        spread[block * block_rows : block * block_rows + slab] = table[block * slab : (block + 1) * slab]
    return spread


def spread_planes(table, blocks, slab):
    planes = round_up(slab, CHUNK) // CHUNK * ROWS
    spread = np.zeros((blocks * planes, table.shape[1]))
    for plane in range(blocks * slab):
        block, own = divmod(plane, slab)
        spread[block * planes + own // CHUNK * ROWS + own % CHUNK] = table[plane]
    return spread


def folded_squares(indices, grid_size):
    folded = jnp.minimum(indices, grid_size - indices).astype(F32)
    return folded * folded


def sine_of_half_turns(turns):
    angle = turns * jnp.pi
    square = angle * angle
    series = jnp.full_like(square, 1.0 / 6227020800.0)
    for factor in (-1.0 / 39916800.0, 1.0 / 362880.0, -1.0 / 5040.0, 1.0 / 120.0, -1.0 / 6.0, 1.0):
        series = series * square + factor
    return angle * series


def truncated_kernel(grid_size, slab, rows):
    lanes = folded_squares(jnp.minimum(jnp.arange(LANES, dtype=jnp.int32), grid_size), grid_size)
    folded = jnp.arange(round_up(grid_size // 2 + 1, 8), dtype=jnp.int32).astype(F32)
    squares = folded * folded
    own_rows = lax.axis_index("fft") * slab + jnp.arange(rows, dtype=jnp.int32)
    row_squares = folded_squares(own_rows, grid_size)
    summed = row_squares[:, None, None] + squares[None, :, None] + lanes[None, None, :]
    safe_sum = jnp.maximum(summed, 1.0)
    half_radius = 0.5 * jnp.sqrt(safe_sum)
    sine = sine_of_half_turns(half_radius - jnp.round(half_radius))
    profile = jnp.where(summed > 0.5, 4.0 * sine * sine / (jnp.pi * jnp.pi * safe_sum), 1.0)
    return profile * (0.25 / float(grid_size) ** 1.5)


def parts_of(value):
    high = value.astype(BF16)
    return high, (value - high.astype(F32)).astype(BF16)


def dot(left, right):
    return jnp.dot(left, right, preferred_element_type=F32)


def times_table(value, table):
    high, low = parts_of(value)
    return dot(jnp.concatenate([high, low, high], axis=1), table)


def table_times(table, value):
    high, low = parts_of(value)
    return dot(table, jnp.concatenate([high, low, high], axis=0))


def exponent_of(largest):
    return jnp.ceil(jnp.log2(jnp.maximum(largest, 1e-30)) * STEPS_PER_OCTAVE)


def step_of(exponent):
    return jnp.exp2(exponent * (1.0 / STEPS_PER_OCTAVE))


def coded(value):
    exponent = exponent_of(jnp.max(jnp.abs(value), axis=-2, keepdims=True))
    scaled = jnp.round(value * (LEVELS / step_of(exponent)))
    row = lax.broadcasted_iota(jnp.int32, value.shape, value.ndim - 2)
    return jnp.where(row == CHUNK, exponent, scaled)


def decoded(code):
    return code * (step_of(code[..., CHUNK:, :]) * (1.0 / LEVELS))


def to_wire(code):
    return code.astype(jnp.int32).astype(jnp.int16)


def from_wire(wire):
    return wire.astype(jnp.int32).astype(F32)


def shared_lanes(first, second):
    lane = lax.broadcasted_iota(jnp.int32, first.shape, first.ndim - 1)
    return jnp.where(lane < 64, first, pltpu.roll(second, 64, second.ndim - 1))


def unshared(both):
    lane = lax.broadcasted_iota(jnp.int32, both.shape, both.ndim - 1)
    first = jnp.where(lane < 64, both, 0.0)
    second = jnp.where(lane < 64, pltpu.roll(both, 64, both.ndim - 1), 0.0)
    return first, second


def group_slices(group_lanes, grid_size):
    for row in range(group_lanes // grid_size):
        first, offset = divmod(row * grid_size, 128)
        yield row, first, offset, -(-(offset + grid_size) // 128)


def forward_kernel(blocks, block_rows, a_ref, b_ref, z_ref, y_ref, out_ref, rows_z, rows_y, buf):
    cells = a_ref.shape[1]
    grid_size = rows_z.shape[0]
    half = out_ref.shape[1] // 3
    group_lanes = 8 * grid_size
    z_table, y_table = z_ref[...], y_ref[...]

    @pl.loop(0, cells // group_lanes, unroll=2)
    def _(group):
        lanes = pl.ds(pl.multiple_of(group * group_lanes, 128), group_lanes)
        flat = a_ref[:, lanes].astype(F32) * b_ref[:, lanes].astype(F32)
        for row, first, offset, tiles in group_slices(group_lanes, grid_size):
            window = flat[:, first * 128 : (first + tiles) * 128]
            if offset:
                window = pltpu.roll(window, tiles * 128 - offset, 1)
            rows_z[group * 8 + row] = window[:, :LANES]

    @pl.loop(0, 2)
    def _(part):
        count = grid_size // 2
        at = pl.ds(pl.multiple_of(part * count, 8), count)
        along_z = times_table(rows_z[at].reshape(count * ROWS, LANES), z_table)
        rows_y[:, at, :] = jnp.transpose(along_z.reshape(count, ROWS, LANES), (1, 0, 2))

    @pl.loop(0, 2)
    def _(part):
        along_y = jnp.stack([table_times(y_table, rows_y[part * 8 + i]) for i in range(8)])
        at = pl.ds(pl.multiple_of(part * 8, 8), 8)
        buf[:, at, :] = jnp.transpose(along_y, (1, 0, 2))

    @pl.loop(0, half)
    def _(row):
        for block in range(blocks):
            first = coded(buf[block * block_rows + row])
            second = coded(buf[block * block_rows + half + row])
            out_ref[block, row] = to_wire(first[:, :128])
            out_ref[block, half + row] = to_wire(second[:, :128])
            out_ref[block, 2 * half + row] = to_wire(shared_lanes(first[:, 128:], second[:, 128:]))


def filter_kernel(chunks, *refs):
    in_refs, (w_ref, forward_ref, inverse_ref, out_ref) = refs[:chunks], refs[chunks:]
    blocks, half = out_ref.shape[0], out_ref.shape[1] // 3
    middle = forward_ref.shape[0] // 2
    forward, inverse = forward_ref[...], inverse_ref[...]

    @pl.loop(0, half, unroll=2)
    def _(row):
        upper = [unshared(from_wire(ref[:, 2 * half + row])) for ref in in_refs]
        codes = []
        for i in range(2):
            at = row + i * half
            fields = [
                decoded(jnp.concatenate([from_wire(ref[:, at]), upper[chunk][i]], axis=-1))
                for chunk, ref in enumerate(in_refs)
            ]
            field = jnp.concatenate(fields, axis=1).reshape(blocks * chunks * ROWS, LANES)
            lower_w = w_ref[at, :middle]
            rows = lax.broadcasted_iota(jnp.int32, lower_w.shape, 0)
            upper_w = jnp.where(rows == 0, w_ref[at, middle : middle + 1], lower_w)
            spectrum = table_times(forward, field) * jnp.concatenate([lower_w, upper_w], axis=0)
            filtered = table_times(inverse, spectrum).reshape(blocks, chunks, ROWS, LANES)
            code = coded(filtered).reshape(blocks, chunks * ROWS, LANES)
            out_ref[:, at] = to_wire(code[..., :128])
            codes.append(code[..., 128:])
        out_ref[:, 2 * half + row] = to_wire(shared_lanes(codes[0], codes[1]))


def back_kernel(blocks, block_rows, adding, in_ref, a_ref, b_ref, occ, z_ref, y_ref, *refs):
    own_ref, ret_ref, buf, rows_z, field = refs[adding:]
    cells = a_ref.shape[1]
    grid_size = rows_z.shape[0]
    half = in_ref.shape[1] // 3
    group_lanes = 8 * grid_size
    z_table, y_table = z_ref[...], y_ref[...]
    home = -0.5 * occ[0]

    for block in range(blocks):
        base = block * block_rows
        buf[base + 2 * half : base + block_rows] = jnp.zeros((block_rows - 2 * half, ROWS, LANES), F32)

    @pl.loop(0, half)
    def _(row):
        for block in range(blocks):
            base = block * block_rows
            upper = unshared(from_wire(in_ref[block, 2 * half + row]))
            for i in range(2):
                at = row + i * half
                code = jnp.concatenate([from_wire(in_ref[block, at]), upper[i]], axis=-1)
                buf[base + at] = decoded(code)

    @pl.loop(0, 2)
    def _(part):
        rows = pl.ds(pl.multiple_of(part * 8, 8), 8)
        mixed = jnp.transpose(buf[:, rows, :], (1, 0, 2))
        along_y = jnp.stack([table_times(y_table, mixed[i]) for i in range(8)])
        along_z = times_table(along_y.reshape(8 * grid_size, LANES), z_table)
        rows_z[...] = jnp.transpose(along_z.reshape(8, grid_size, LANES), (1, 0, 2))

        @pl.loop(0, cells // group_lanes, unroll=2)
        def _(group):
            tiles_of = [None] * (group_lanes // 128)
            for row, first, offset, tiles in group_slices(group_lanes, grid_size):
                window = rows_z[group * 8 + row]
                if tiles * 128 > LANES:
                    window = jnp.concatenate([window, jnp.zeros((8, tiles * 128 - LANES), F32)], axis=1)
                if offset:
                    window = pltpu.roll(window, offset, 1)
                for tile in range(tiles):
                    piece = window[:, tile * 128 : (tile + 1) * 128]
                    before = tiles_of[first + tile]
                    tiles_of[first + tile] = piece if before is None else before + piece
            lanes = pl.ds(pl.multiple_of(group * group_lanes, 128), group_lanes)
            field[rows, lanes] = jnp.concatenate(tiles_of, axis=1)

    @pl.loop(0, cells // group_lanes)
    def _(group):
        lanes = pl.ds(pl.multiple_of(group * group_lanes, 128), group_lanes)
        potential = field[:, lanes]
        visitor = b_ref[:, lanes].astype(F32)
        own_ref[:, lanes] = potential * visitor * (-0.5 * visitor[CHUNK:])
        terms = potential * a_ref[:, lanes].astype(F32) * home
        if adding:
            terms = terms + decoded(from_wire(refs[0][:, lanes])) * occ[1]
        ret_ref[:, lanes] = to_wire(coded(terms))


def total_kernel(far_own, near_own, far_arrived, near_arrived, flags, *refs):
    out_ref = refs[-1]
    total = far_own[...] + near_own[...]
    total = total + decoded(from_wire(far_arrived[...])) + decoded(from_wire(near_arrived[...])) * flags[2]
    out_ref[:, 0, :] = total[: out_ref.shape[0]]


def call(kernel, out_shape, scratch, name, flops, operands, in_specs=None):
    single = pl.BlockSpec(memory_space=pltpu.VMEM)
    bytes_moved = sum(o.size * o.dtype.itemsize for o in operands)
    return pl.pallas_call(
        kernel,
        grid=(1,) if in_specs else (),
        out_shape=out_shape,
        in_specs=in_specs or [single] * len(operands),
        out_specs=[single] * len(out_shape) if isinstance(out_shape, list) else single,
        scratch_shapes=scratch,
        compiler_params=pltpu.CompilerParams(vmem_limit_bytes=VMEM_BYTES),
        cost_estimate=pl.CostEstimate(flops=flops, bytes_accessed=bytes_moved, transcendentals=0),
        name=name,
    )(*operands)


def exchange(wire):
    return lax.all_to_all(wire, "fft", split_axis=0, concat_axis=0, tiled=True)


def shards(wavefunctions, band_occ):
    _, slab, cells = wavefunctions.shape
    blocks = lax.axis_size("fft")
    bands = lax.axis_size("band")
    grid_size = slab * blocks
    chunks = round_up(slab, CHUNK) // CHUNK
    planes = chunks * ROWS
    block_rows = round_up(slab, 8)
    half = (slab + 1) // 2
    ky_rows = blocks * block_rows

    table = cas_table(grid_size)
    square_table = np.zeros((LANES, LANES))
    square_table[:grid_size, :grid_size] = table
    to_ky = spread_rows(table, blocks, slab, block_rows)
    middle = grid_size // 2
    kx_order = np.concatenate([np.arange(middle), [middle], grid_size - np.arange(1, middle)])
    to_x = spread_planes(table[:, kx_order], blocks, slab)
    z_table = high_low(square_table, 0)
    y_forward, y_back = high_low(to_ky, 1), high_low(to_ky.T, 1)
    x_forward, x_back = high_low(to_x.T, 1), high_low(to_x, 1)
    profile = truncated_kernel(grid_size, slab, 2 * half)

    occupied = band_occ.astype(BF16)
    upward = [(i, (i + 2) % bands) for i in range(bands)]
    downward = [(i, (i - 2) % bands) for i in range(bands)]
    swap = [(i, i ^ 1) for i in range(bands)]
    is_odd = lax.axis_index("band") % 2 == 1

    def chunk_of(chunk):
        piece = wavefunctions[0, chunk * CHUNK : (chunk + 1) * CHUNK]
        return jnp.pad(piece, ((0, ROWS - piece.shape[0]), (0, 0)))

    home = [chunk_of(chunk) for chunk in range(chunks)]
    spare_row = jnp.arange(ROWS, dtype=jnp.int32)[:, None] == CHUNK
    carrying = [jnp.where(spare_row, occupied, piece) for piece in home]
    far, near = [], []
    for chunk in range(chunks):
        sent = carrying[chunk]
        far.append(lax.ppermute(sent, "band", upward))
    far[0], profile = lax.optimization_barrier((far[0], profile))
    for chunk in range(chunks):
        near.append(lax.ppermute(jnp.where(is_odd, far[chunk], carrying[chunk]), "band", swap))
    flops = 12 * ROWS * grid_size**3

    def forward(chunk, visitor):
        return call(
            functools.partial(forward_kernel, blocks, block_rows),
            jax.ShapeDtypeStruct((blocks, 3 * half, ROWS, 128), jnp.int16),
            [
                pltpu.VMEM((grid_size, ROWS, LANES), F32),
                pltpu.VMEM((ROWS, grid_size, LANES), F32),
                pltpu.VMEM((ky_rows, ROWS, LANES), F32),
            ],
            "density_to_ky_kz",
            flops,
            [home[chunk], visitor[chunk], z_table, y_forward],
        )

    def filtered(wires):
        return call(
            functools.partial(filter_kernel, chunks),
            jax.ShapeDtypeStruct((blocks, 3 * half, planes, 128), jnp.int16),
            [],
            "filter_along_x",
            chunks * flops,
            [*wires, profile, x_forward, x_back],
        )

    def back(wire, chunk, visitor, factors, added=()):
        whole = pl.BlockSpec(memory_space=pltpu.VMEM)
        piece = pl.BlockSpec((blocks, 3 * half, ROWS, 128), lambda i: (0, 0, chunk, 0))
        return call(
            functools.partial(back_kernel, blocks, block_rows, len(added)),
            [
                jax.ShapeDtypeStruct((ROWS, cells), F32),
                jax.ShapeDtypeStruct((ROWS, cells), jnp.int16),
            ],
            [
                pltpu.VMEM((ky_rows, ROWS, LANES), F32),
                pltpu.VMEM((grid_size, 8, LANES), F32),
                pltpu.VMEM((ROWS, cells), F32),
            ],
            "potential_terms",
            flops,
            [wire, home[chunk], visitor[chunk], factors, z_table, y_back, *added],
            [piece, whole, whole, pl.BlockSpec(memory_space=pltpu.SMEM)] + [whole] * (2 + len(added)),
        )

    odd = is_odd.astype(F32)
    factors = flags = jnp.stack([occupied.astype(F32)[0], odd, 1.0 - odd])

    far_wires = [exchange(forward(chunk, far)) for chunk in range(chunks)]
    near_wires = [exchange(forward(chunk, near)) for chunk in range(chunks)]
    near_wire = exchange(filtered(near_wires))
    far_wire = exchange(filtered(far_wires))
    near_own, crossed, far_own, arrived = [], [], [], []
    for chunk in range(chunks):
        own, terms = back(near_wire, chunk, near, factors)
        factors, terms = lax.optimization_barrier((factors, terms))
        near_own.append(own)
        crossed.append(lax.ppermute(terms, "band", swap))
    for chunk in range(chunks):
        if chunk >= 2:
            factors, arrived[chunk - 2] = lax.optimization_barrier((factors, arrived[chunk - 2]))
        own, terms = back(far_wire, chunk, far, factors, [crossed[chunk]])
        factors, terms = lax.optimization_barrier((factors, terms))
        far_own.append(own)
        arrived.append(lax.ppermute(terms, "band", downward))
    width = 16 * grid_size
    spec = pl.BlockSpec((ROWS, width), lambda i: (0, i))
    result = None
    for chunk in range(chunks):
        operands = [far_own[chunk], near_own[chunk], arrived[chunk], crossed[chunk], flags]
        started = [] if result is None else [result]
        result = pl.pallas_call(
            total_kernel,
            grid=(cells // width,),
            out_shape=jax.ShapeDtypeStruct((slab, 1, cells), F32),
            in_specs=[spec] * 4 + [pl.BlockSpec(memory_space=pltpu.SMEM)] + [pl.BlockSpec(memory_space=pl.ANY)] * len(started),
            out_specs=pl.BlockSpec((min(CHUNK, slab), 1, width), functools.partial(lambda at, i: (at, 0, i), chunk)),
            input_output_aliases={5: 0} if started else {},
            compiler_params=pltpu.CompilerParams(vmem_limit_bytes=VMEM_BYTES),
            name="total_terms",
        )(*operands, *started)
    return result.reshape(1, slab, cells)


def solution(mesh):
    in_specs = (P("band", "fft", None), P("band"))
    out_specs = P("band", "fft", None)
    return jax.shard_map(shards, mesh=mesh, in_specs=in_specs, out_specs=out_specs, check_vma=False)
```
